32 devices in a mesh: sub: 16 (over z, y, x), coarse: 2 (over core).
Axes of the slice: x: 2, y: 2, z: 4, core: 2. Of those that a mesh axis runs over, the one named last changes fastest.
Arguments:
- right_side: float32 [16, 64, 256], P('sub', None, 'coarse'), may hold values from -6 to 6
- local_blocks: bfloat16 [16, 2, 64, 64, 256], P('sub', None, None, None, 'coarse'), may hold values from -0.5 to 0.5
- diag_blocks: bfloat16 [16, 64, 64, 256], P('sub', None, None, 'coarse'), as said below
- iface_blocks: bfloat16 [16, 64, 64, 192], P('sub', None, None, 'coarse'), may hold values from -0.75 to 0.75
- block_cols: int32 [16, 2, 256], P('sub', None, 'coarse'), may hold values from 0 to 255
- basis: bfloat16 [16, 32, 64, 256], P('sub', None, None, 'coarse'), may hold values from -0.09375 to 0.09375
- coarse_inverse: float32 [512, 512], P('sub'), as said below
Outputs:
- solution_field: float32 [16, 64, 256], P('sub', None, 'coarse')
- residual: float32 [16, 64, 256], P('sub', None, 'coarse')
The draws below stay inside these ranges and needn't reach their ends.
Inputs may be any that keep to these rules, and one draw needn't show every extreme that they name: `diag_blocks`: each diagonal block is 4 times the identity plus entries of magnitude at most 0.5. `coarse_inverse`: the matrix is the identity plus entries of magnitude at most 4 / sqrt(512).
All inputs are finite; a program needn't handle non-finite values.
Results may differ from the reference program's by a relative error of at most 0.0003.
Values sent between devices are 32-bit elements; how exact they have to be, the bound alone decides.
No kernel may reach another device: no remote copies, remote signals or barrier semaphores. Data moves between devices by JAX's collectives and lax.ppermute only.
A program may use at most 64 MiB of HBM per device.

```python
import jax
import jax.numpy as jnp
from jax import lax

B = 64
NV = 32
K = 2
SWEEPS = 3
ITERS = 2
RB = 128
IB = 32
ROWBLOCKS = 256
SUBS = 16
CDIM = 512
N_COARSE = 2


def draw_diag_blocks(key, part):
    noise = jnp.clip(jax.random.normal(key, (SUBS, B, B, ROWBLOCKS), jnp.float32), -4.0, 4.0) * 0.125
    eye = jnp.eye(B, dtype=jnp.float32)[None, :, :, None]
    return (4.0 * eye + noise).astype(jnp.bfloat16)


def draw_coarse_inverse(key, part):
    noise = jnp.clip(jax.random.normal(key, (CDIM, CDIM), jnp.float32), -4.0, 4.0) * CDIM ** (-0.5)
    return jnp.eye(CDIM, dtype=jnp.float32) + noise


def plant(result, rng, smallest, top_value):
    longest = result.shape.index(max(result.shape))
    spots = []
    for shift in (0, 1):
        where = [jax.random.randint(jax.random.fold_in(rng, axis), (), 0, length) for axis, length in enumerate(result.shape)]
        where[longest] = (where[longest] + shift) % result.shape[longest]
        spots.append(tuple(where))
    return result.at[spots[0]].set(smallest).at[spots[1]].set(top_value)


def levels(own_key, shape, shards, low, top_value):
    gain, own = 1.0, jax.random.fold_in(own_key, 6)
    for position, shards_of in shards:
        draws = jnp.exp(jax.random.uniform(jax.random.fold_in(own, position), (shards_of,), jnp.float32, low / len(shards), top_value / len(shards)))
        gain = gain * jnp.repeat(draws, shape[position] // shards_of).reshape([-1 if axis == position else 1 for axis in range(len(shape))])
    return gain


def bell_draw(own_key, shape, scale, most, pieces=(), held_as=jnp.bfloat16):
    array = scale * jax.random.normal(own_key, shape, jnp.float32)
    if pieces:
        array = array * levels(own_key, shape, pieces, -0.22, 0.18)
    return jnp.clip(array, -most, most).astype(held_as)


def setup_inputs(seed: int = 0) -> dict:
    keys = jax.random.split(jax.random.key(seed), 8)
    right_side = bell_draw(keys[0], (SUBS, B, ROWBLOCKS), 1.0, 6.0, ((0, 16), (2, 2)), jnp.float32)
    local_blocks = bell_draw(keys[1], (SUBS, K, B, B, ROWBLOCKS), (B * K) ** -0.5, 0.5, ((0, 16), (4, 2)))
    diag_blocks = draw_diag_blocks(jax.random.fold_in(keys[7], 71), 0)
    iface_blocks = bell_draw(keys[3], (SUBS, B, B, N_COARSE * 3 * IB), B ** -0.5, 0.75, ((0, 16), (3, 2)))
    block_cols = plant(jax.random.randint(keys[4], (SUBS, K, ROWBLOCKS), 0, ROWBLOCKS), jax.random.fold_in(keys[4], 1), 0, ROWBLOCKS - 1).astype(jnp.int32)
    basis = bell_draw(keys[5], (SUBS, NV, B, ROWBLOCKS), (2.0 / (B * ROWBLOCKS) ** 0.5), 0.09375, ((0, 16), (3, 2)))
    coarse_inverse = draw_coarse_inverse(jax.random.fold_in(keys[7], 71), 0)
    return {"right_side": right_side, "local_blocks": local_blocks, "diag_blocks": diag_blocks, "iface_blocks": iface_blocks, "block_cols": block_cols, "basis": basis, "coarse_inverse": coarse_inverse}


HIGH = lax.Precision.HIGHEST


def local_product(lblocks, dblock, cols, vec):
    picked = vec[:, cols]
    off = jnp.einsum('kijr,jkr->ir', lblocks.astype(jnp.float32), picked, precision=HIGH)
    own = jnp.einsum('ijr,jr->ir', dblock.astype(jnp.float32), vec, precision=HIGH)
    return own + off


def relax(dblock, vec):
    return 0.25 * (2.0 * vec - 0.25 * jnp.einsum('ijr,jr->ir', dblock.astype(jnp.float32), vec, precision=HIGH))


def reference(right_side, local_blocks, diag_blocks, iface_blocks, block_cols, basis, coarse_inverse):
    count = right_side.shape[2] // RB
    inner = iface_blocks.shape[3] // (3 * count)
    index = jnp.arange(SUBS, dtype=jnp.int32)

    def full_product(vec):
        partners = [vec[jnp.bitwise_xor(index, 1 << q)] for q in range(3)]

        def one(items):
            lblocks, dblock, fblock, cols, own, part0, part1, part2 = items
            out = local_product(lblocks, dblock, cols, own).reshape(B, count, RB)
            fshaped = fblock.astype(jnp.float32).reshape(B, B, count, 3, inner)
            for q, part in enumerate((part0, part1, part2)):
                near = part.reshape(B, count, RB)[:, :, q * inner:(q + 1) * inner]
                add = jnp.einsum('ijcm,jcm->icm', fshaped[:, :, :, q, :], near, precision=HIGH)
                out = out.at[:, :, q * inner:(q + 1) * inner].add(add)
            return out.reshape(B, count * RB)

        return lax.map(one, (local_blocks, diag_blocks, iface_blocks, block_cols, vec, partners[0], partners[1], partners[2]))

    def smooth(resid):
        def one(items):
            lblocks, dblock, cols, piece = items
            state = relax(dblock, piece)
            for sweep in range(SWEEPS - 1):
                state = state + relax(dblock, piece - local_product(lblocks, dblock, cols, state))
            return state
        return lax.map(one, (local_blocks, diag_blocks, block_cols, resid))

    def coarse(resid):
        def restrict(items):
            zvec, piece = items
            return jnp.einsum('vjr,jr->v', zvec.astype(jnp.float32), piece, precision=HIGH)
        proj = lax.map(restrict, (basis, resid))
        coeff = jnp.dot(coarse_inverse, proj.reshape(-1), precision=HIGH).reshape(SUBS, -1)

        def extend(items):
            zvec, weights = items
            return jnp.einsum('v,vjr->jr', weights, zvec.astype(jnp.float32), precision=HIGH)
        return lax.map(extend, (basis, coeff))

    solution_field = jnp.zeros_like(right_side)
    residual = right_side
    for step in range(ITERS):
        direction = smooth(residual) + coarse(residual)
        image = full_product(direction)
        alpha = jnp.sum(residual * image) / (jnp.sum(image * image) + 1e-6)
        solution_field = solution_field + alpha * direction
        residual = residual - alpha * image
    return solution_field, residual
```

```python
import functools

import jax
import jax.numpy as jnp
from jax import lax
from jax.experimental import pallas as pl
from jax.experimental.pallas import tpu as pltpu
from jax.sharding import PartitionSpec as P

SWEEPS = 3
ITERS = 2
ROWS = 8
HIGH = lax.Precision.HIGHEST


def in_vmem(array):
    return pltpu.with_memory_space_constraint(array, pltpu.VMEM)


def call(body, outs, *args, macs=0):
    args = [in_vmem(a) for a in args]
    size = sum(a.size * a.dtype.itemsize for a in args)
    return pl.pallas_call(
        body,
        out_shape=[pltpu.VMEM(shape, jnp.float32) for shape in outs],
        in_specs=[pl.BlockSpec(memory_space=pltpu.VMEM) for _ in args],
        out_specs=[pl.BlockSpec(memory_space=pltpu.VMEM) for _ in outs],
        cost_estimate=pl.CostEstimate(flops=2 * macs, bytes_accessed=size, transcendentals=0),
    )(*args)


def rows_times(blocks, vec, start):
    chunk = blocks[pl.ds(start, ROWS)].astype(jnp.float32)
    return jnp.sum(chunk * vec[None], axis=1)


def by_rows(count, body):
    def step(at, carry):
        body(pl.multiple_of(at * ROWS, ROWS))
        return carry

    lax.fori_loop(0, count // ROWS, step, 0)


def block_product(blocks, vec, out):
    def body(start):
        out[pl.ds(start, ROWS), :] = rows_times(blocks, vec, start)

    by_rows(blocks.shape[0], body)


def relaxed(dblock, vec, out, base=None):
    def body(start):
        part = dblock_rows(dblock, vec, start)
        value = part if base is None else base[pl.ds(start, ROWS), :] + part
        out[pl.ds(start, ROWS), :] = value

    whole = vec[...]

    def dblock_rows(blocks, ref, start):
        return 0.25 * (2.0 * ref[pl.ds(start, ROWS), :] - 0.25 * rows_times(blocks, whole, start))

    by_rows(dblock.shape[0], body)


def restricted(zvec, vec, scratch, sub):
    block_product(zvec, vec, scratch)
    nvec = scratch.shape[0]
    lanes = scratch.shape[1]
    copies = lanes // nvec
    part = scratch[...]
    stacked = jnp.concatenate([part] * copies, axis=0)
    ones = jnp.ones((8, lanes), jnp.float32)
    sums = lax.dot_general(
        ones, stacked, (((1,), (1,)), ((), ())), precision=HIGH, preferred_element_type=jnp.float32
    )
    lane = lax.broadcasted_iota(jnp.int32, sums.shape, 1)
    row = lax.broadcasted_iota(jnp.int32, sums.shape, 0)
    keep = (lane // nvec == lax.rem(sub, copies)) & (row == 0)
    return jnp.where(keep, sums, 0.0)


def spread(message, cross, square):
    row = lax.broadcasted_iota(jnp.int32, message.shape, 0)
    return jnp.where(row == 1, cross, jnp.where(row == 2, square, message))


def total(x):
    return jnp.sum(x, keepdims=True)


def first_kernel(resid, dblock, zvec, state, message, scratch):
    relaxed(dblock, resid, state)
    message[...] = jnp.broadcast_to(
        restricted(zvec, resid[...], scratch, lax.axis_index("sub"))[None], message.shape
    )


def diag_kernel(vec, dblock, out):
    block_product(dblock, vec[...], out)


def picked(vec, others, cols, part):
    me = lax.axis_index("coarse")
    width = vec.shape[1]
    index = jnp.broadcast_to(cols[pl.ds(part, 1), :], vec.shape)
    owner = index // width
    place = lax.rem(index, width)

    def lanes(block):
        return jnp.take_along_axis(block, place, axis=1, mode="promise_in_bounds")

    if others.shape[0] == 1:
        return jnp.where(owner == me, lanes(vec[...]), lanes(others[0]))
    value = lanes(others[0])
    for at in range(1, others.shape[0]):
        value = jnp.where(owner == at, lanes(others[at]), value)
    return value


def off_rows(lblocks, chosen, start):
    value = rows_times(lblocks.at[0], chosen[0], start)
    for part in range(1, len(chosen)):
        value = value + rows_times(lblocks.at[part], chosen[part], start)
    return value


def sweep_kernel(state, others, own, resid, dblock, lblocks, cols, out, rest):
    chosen = [picked(state, others, cols, part) for part in range(lblocks.shape[0])]

    def body(start):
        here = pl.ds(start, ROWS)
        rest[here, :] = resid[here, :] - (own[here, :] + off_rows(lblocks, chosen, start))

    by_rows(dblock.shape[0], body)
    relaxed(dblock, rest, out, state)


def off_kernel(vec, others, own, lblocks, cols, out):
    chosen = [picked(vec, others, cols, part) for part in range(lblocks.shape[0])]

    def body(start):
        out[pl.ds(start, ROWS), :] = own[pl.ds(start, ROWS), :] + off_rows(lblocks, chosen, start)

    by_rows(out.shape[0], body)


def step_size(arrived):
    cross = jnp.sum(arrived[:, 1, :], axis=0, keepdims=True)
    square = jnp.sum(arrived[:, 2, :], axis=0, keepdims=True)
    return cross / (square + 1e-06)


def corrected(state, arrived, inverse, zvec, count):
    nvec = zvec.shape[0]
    lanes = state.shape[1]
    each = count * (lanes // nvec)
    acc = jnp.zeros((nvec, lanes), jnp.float32)
    for at in range(inverse.shape[1] // lanes):
        row = jnp.sum(arrived[at * each : (at + 1) * each, 0, :], axis=0, keepdims=True)
        acc = acc + inverse[:, at * lanes : (at + 1) * lanes] * row
    weights = jnp.broadcast_to(jnp.sum(acc, axis=1, keepdims=True), acc.shape)
    value = state[...]
    for at in range(nvec):
        value = value + weights[at : at + 1, :] * zvec[at].astype(jnp.float32)
    return value


def direction_kernel(count, state, arrived, inverse, zvec, out):
    out[...] = corrected(state, arrived, inverse, zvec, count)


def next_direction_kernel(count, state, arrived, inverse, zvec, previous, resid, image, out, rest, alpha):
    size = step_size(arrived)
    out[...] = previous[...] - size * corrected(state, arrived, inverse, zvec, count)
    rest[...] = resid[...] - size * image[...]
    alpha[...] = jnp.broadcast_to(size, alpha.shape)


def near(parts, inner):
    lane = lax.broadcasted_iota(jnp.int32, parts[0].shape, 1)
    value = parts[0][...]
    for at in range(1, len(parts)):
        value = jnp.where(lane < at * inner, value, parts[at][...])
    return value[:, : len(parts) * inner]


def with_interface(known, parts, fblock, out):
    width = fblock.shape[2]
    vec = near(parts, width // len(parts))

    def body(start):
        here = pl.ds(start, ROWS)
        add = rows_times(fblock, vec, start)
        pad = jnp.zeros((ROWS, out.shape[1] - width), jnp.float32)
        out[here, :] = known[here, :] + jnp.concatenate([add, pad], axis=1)

    by_rows(out.shape[0], body)


def image_kernel(known, near0, near1, near2, fblock, resid, dblock, zvec, image, state, message, scratch):
    with_interface(known, (near0, near1, near2), fblock, image)
    relaxed(dblock, image, state)
    value = image[...]
    row = restricted(zvec, value, scratch, lax.axis_index("sub"))
    row = spread(row, total(resid[...] * value), total(value * value))
    message[...] = jnp.broadcast_to(row[None], message.shape)


def last_image_kernel(known, near0, near1, near2, fblock, resid, image, message):
    with_interface(known, (near0, near1, near2), fblock, image)
    value = image[...]
    row = spread(jnp.zeros(message.shape[1:], jnp.float32), total(resid[...] * value), total(value * value))
    message[...] = jnp.broadcast_to(row[None], message.shape)


def final_kernel(arrived, alpha, first, second, resid, image, field, rest):
    size = step_size(arrived)
    field[...] = alpha[0:1, :] * first[...] + size * second[...]
    rest[...] = resid[...] - size * image[...]


def swap(count, apart):
    return [(low, low ^ apart) for low in range(count) if low ^ apart < count]


def gathered(vec, count):
    if count == 2:
        return lax.ppermute(vec, "coarse", swap(2, 1))[None]
    return lax.all_gather(vec, "coarse", axis=0)


def local(subs, count, right_side, local_blocks, diag_blocks, iface_blocks, block_cols, basis, coarse_inverse):
    lblocks, dblock, fblock = local_blocks[0], diag_blocks[0], iface_blocks[0]
    cols, zvec, resid = block_cols[0], basis[0], right_side[0]
    shape = resid.shape
    devices = subs * count
    parcel = (devices, 8, shape[1])
    scratch = (zvec.shape[0], shape[1])
    lblocks, dblock, fblock, zvec, inverse = map(in_vmem, (lblocks, dblock, fblock, zvec, coarse_inverse))
    resid, cols = in_vmem(resid), in_vmem(cols)

    def everywhere(message):
        return lax.all_to_all(message, ("sub", "coarse"), 0, 0)

    def smooth(resid, state):
        for sweep in range(SWEEPS - 1):
            others = gathered(state, count)
            (own,) = call(diag_kernel, [shape], state, dblock, macs=dblock.size)
            state, _ = call(
                sweep_kernel, [shape, shape], state, others, own, resid, dblock, lblocks, cols,
                macs=dblock.size + lblocks.size,
            )
        return state

    def apply(vec):
        others = gathered(vec, count)
        near_parts = [lax.ppermute(vec, "sub", swap(subs, 1 << bit)) for bit in range(3)]
        (own,) = call(diag_kernel, [shape], vec, dblock, macs=dblock.size)
        (known,) = call(off_kernel, [shape], vec, others, own, lblocks, cols, macs=lblocks.size)
        return [known, *near_parts, fblock]

    state, message, _ = call(
        first_kernel, [shape, parcel, scratch], resid, dblock, zvec, macs=dblock.size + zvec.size
    )
    arrived = everywhere(message)
    state = smooth(resid, state)
    (first,) = call(
        functools.partial(direction_kernel, count), [shape], state, arrived, inverse, zvec, macs=zvec.size
    )
    image, state, message, _ = call(
        image_kernel, [shape, shape, parcel, scratch], *apply(first), resid, dblock, zvec,
        macs=dblock.size + zvec.size + fblock.size,
    )
    arrived = everywhere(message)
    state = smooth(image, state)
    second, rest, alpha = call(
        functools.partial(next_direction_kernel, count), [shape, shape, (8, shape[1])],
        state, arrived, inverse, zvec, first, resid, image, macs=zvec.size,
    )
    image, message = call(last_image_kernel, [shape, parcel], *apply(second), rest, macs=fblock.size)
    arrived = everywhere(message)
    field, rest = call(final_kernel, [shape, shape], arrived, alpha, first, second, rest, image)
    return field[None], rest[None]


def solution(mesh):
    placed = (
        P("sub", None, "coarse"),
        P("sub", None, None, None, "coarse"),
        P("sub", None, None, "coarse"),
        P("sub", None, None, "coarse"),
        P("sub", None, "coarse"),
        P("sub", None, None, "coarse"),
        P("sub", None),
    )
    return jax.shard_map(
        functools.partial(local, mesh.shape["sub"], mesh.shape["coarse"]),
        mesh=mesh,
        in_specs=placed,
        out_specs=(P("sub", None, "coarse"), P("sub", None, "coarse")),
        check_vma=False,
    )
```

```python
import functools

import jax
import jax.numpy as jnp
from jax import lax
from jax.experimental import pallas as pl
from jax.experimental.pallas import tpu as pltpu
from jax.sharding import PartitionSpec as P

SWEEPS = 3
ITERS = 2
ROWS = 8
SCOPED = 2 << 20
HIGH = lax.Precision.HIGHEST


def in_vmem(array):
    return pltpu.with_memory_space_constraint(array, pltpu.VMEM)


def call(body, outs, *args, macs=0):
    args = [in_vmem(a) for a in args]
    size = sum(a.size * a.dtype.itemsize for a in args)
    return pl.pallas_call(
        body,
        out_shape=[pltpu.VMEM(shape, jnp.float32) for shape in outs],
        in_specs=[pl.BlockSpec(memory_space=pltpu.VMEM) for _ in args],
        out_specs=[pl.BlockSpec(memory_space=pltpu.VMEM) for _ in outs],
        cost_estimate=pl.CostEstimate(flops=2 * macs, bytes_accessed=size, transcendentals=0),
        compiler_params=pltpu.CompilerParams(vmem_limit_bytes=SCOPED),
    )(*args)


def rows_times(blocks, vec, start):
    chunk = blocks[pl.ds(start, ROWS)].astype(jnp.float32)
    return jnp.sum(chunk * vec[None], axis=1)


def by_rows(count, body):
    def step(at, carry):
        body(pl.multiple_of(at * ROWS, ROWS))
        return carry

    lax.fori_loop(0, count // ROWS, step, 0)


def block_product(blocks, vec, out):
    def body(start):
        out[pl.ds(start, ROWS), :] = rows_times(blocks, vec, start)

    by_rows(blocks.shape[0], body)


def relaxed(dblock, vec, out, base=None):
    def body(start):
        part = dblock_rows(dblock, vec, start)
        value = part if base is None else base[pl.ds(start, ROWS), :] + part
        out[pl.ds(start, ROWS), :] = value

    whole = vec[...]

    def dblock_rows(blocks, ref, start):
        return 0.25 * (2.0 * ref[pl.ds(start, ROWS), :] - 0.25 * rows_times(blocks, whole, start))

    by_rows(dblock.shape[0], body)


def restricted(zvec, vec, scratch, sub):
    block_product(zvec, vec, scratch)
    nvec = scratch.shape[0]
    lanes = scratch.shape[1]
    copies = lanes // nvec
    part = scratch[...]
    stacked = jnp.concatenate([part] * copies, axis=0)
    ones = jnp.ones((8, lanes), jnp.float32)
    sums = lax.dot_general(
        ones, stacked, (((1,), (1,)), ((), ())), precision=HIGH, preferred_element_type=jnp.float32
    )
    lane = lax.broadcasted_iota(jnp.int32, sums.shape, 1)
    row = lax.broadcasted_iota(jnp.int32, sums.shape, 0)
    keep = (lane // nvec == lax.rem(sub, copies)) & (row == 0)
    return jnp.where(keep, sums, 0.0)


def spread(message, cross, square):
    row = lax.broadcasted_iota(jnp.int32, message.shape, 0)
    return jnp.where(row == 1, cross, jnp.where(row == 2, square, message))


def total(x):
    return jnp.sum(x, keepdims=True)


def first_kernel(resid, dblock, zvec, state, message, scratch):
    relaxed(dblock, resid, state)
    message[...] = jnp.broadcast_to(
        restricted(zvec, resid[...], scratch, lax.axis_index("sub"))[None], message.shape
    )


def diag_kernel(vec, dblock, out):
    block_product(dblock, vec[...], out)


def picked(vec, others, cols, part):
    me = lax.axis_index("coarse")
    width = vec.shape[1]
    index = jnp.broadcast_to(cols[pl.ds(part, 1), :], vec.shape)
    owner = index // width
    place = lax.rem(index, width)

    def lanes(block):
        return jnp.take_along_axis(block, place, axis=1, mode="promise_in_bounds")

    if others.shape[0] == 1:
        return jnp.where(owner == me, lanes(vec[...]), lanes(others[0]))
    value = lanes(others[0])
    for at in range(1, others.shape[0]):
        value = jnp.where(owner == at, lanes(others[at]), value)
    return value


def off_rows(lblocks, chosen, start):
    value = rows_times(lblocks.at[0], chosen[0], start)
    for part in range(1, len(chosen)):
        value = value + rows_times(lblocks.at[part], chosen[part], start)
    return value


def sweep_kernel(state, others, own, resid, dblock, lblocks, cols, out, rest):
    chosen = [picked(state, others, cols, part) for part in range(lblocks.shape[0])]

    def body(start):
        here = pl.ds(start, ROWS)
        rest[here, :] = resid[here, :] - (own[here, :] + off_rows(lblocks, chosen, start))

    by_rows(dblock.shape[0], body)
    relaxed(dblock, rest, out, state)


def off_kernel(vec, others, own, lblocks, cols, out):
    chosen = [picked(vec, others, cols, part) for part in range(lblocks.shape[0])]

    def body(start):
        out[pl.ds(start, ROWS), :] = own[pl.ds(start, ROWS), :] + off_rows(lblocks, chosen, start)

    by_rows(out.shape[0], body)


def step_size(arrived):
    cross = jnp.sum(arrived[:, 1, :], axis=0, keepdims=True)
    square = jnp.sum(arrived[:, 2, :], axis=0, keepdims=True)
    return cross / (square + 1e-06)


def corrected(state, arrived, inverse, zvec, count):
    nvec = zvec.shape[0]
    lanes = state.shape[1]
    each = count * (lanes // nvec)
    acc = jnp.zeros((nvec, lanes), jnp.float32)
    for at in range(inverse.shape[1] // lanes):
        row = jnp.sum(arrived[at * each : (at + 1) * each, 0, :], axis=0, keepdims=True)
        acc = acc + inverse[:, at * lanes : (at + 1) * lanes] * row
    weights = jnp.broadcast_to(jnp.sum(acc, axis=1, keepdims=True), acc.shape)
    value = state[...]
    for at in range(nvec):
        value = value + weights[at : at + 1, :] * zvec[at].astype(jnp.float32)
    return value


def direction_kernel(count, state, arrived, inverse, zvec, out):
    out[...] = corrected(state, arrived, inverse, zvec, count)


def next_direction_kernel(count, state, arrived, inverse, zvec, previous, resid, image, out, rest, alpha):
    size = step_size(arrived)
    out[...] = previous[...] - size * corrected(state, arrived, inverse, zvec, count)
    rest[...] = resid[...] - size * image[...]
    alpha[...] = jnp.broadcast_to(size, alpha.shape)


def near(parts, inner):
    lane = lax.broadcasted_iota(jnp.int32, parts[0].shape, 1)
    value = parts[0][...]
    for at in range(1, len(parts)):
        value = jnp.where(lane < at * inner, value, parts[at][...])
    return value[:, : len(parts) * inner]


def with_interface(known, parts, fblock, out):
    width = fblock.shape[2]
    vec = near(parts, width // len(parts))

    def body(start):
        here = pl.ds(start, ROWS)
        add = rows_times(fblock, vec, start)
        pad = jnp.zeros((ROWS, out.shape[1] - width), jnp.float32)
        out[here, :] = known[here, :] + jnp.concatenate([add, pad], axis=1)

    by_rows(out.shape[0], body)


def image_kernel(known, near0, near1, near2, fblock, resid, dblock, zvec, image, state, message, scratch):
    with_interface(known, (near0, near1, near2), fblock, image)
    relaxed(dblock, image, state)
    value = image[...]
    row = restricted(zvec, value, scratch, lax.axis_index("sub"))
    row = spread(row, total(resid[...] * value), total(value * value))
    message[...] = jnp.broadcast_to(row[None], message.shape)


def last_image_kernel(known, near0, near1, near2, fblock, resid, image, message):
    with_interface(known, (near0, near1, near2), fblock, image)
    value = image[...]
    row = spread(jnp.zeros(message.shape[1:], jnp.float32), total(resid[...] * value), total(value * value))
    message[...] = jnp.broadcast_to(row[None], message.shape)


def final_kernel(arrived, alpha, first, second, resid, image, field, rest):
    size = step_size(arrived)
    field[...] = alpha[0:1, :] * first[...] + size * second[...]
    rest[...] = resid[...] - size * image[...]


def swap(count, apart):
    return [(low, low ^ apart) for low in range(count) if low ^ apart < count]


def gathered(vec, count):
    if count == 2:
        return lax.ppermute(vec, "coarse", swap(2, 1))[None]
    return lax.all_gather(vec, "coarse", axis=0)


def local(subs, count, right_side, local_blocks, diag_blocks, iface_blocks, block_cols, basis, coarse_inverse):
    lblocks, dblock, fblock = local_blocks[0], diag_blocks[0], iface_blocks[0]
    cols, zvec, resid = block_cols[0], basis[0], right_side[0]
    shape = resid.shape
    devices = subs * count
    parcel = (devices, 8, shape[1])
    scratch = (zvec.shape[0], shape[1])
    lblocks, dblock, fblock, zvec, inverse = map(in_vmem, (lblocks, dblock, fblock, zvec, coarse_inverse))
    resid, cols = in_vmem(resid), in_vmem(cols)

    def everywhere(message):
        return lax.all_to_all(message, ("sub", "coarse"), 0, 0)

    def smooth(resid, state):
        for sweep in range(SWEEPS - 1):
            others = gathered(state, count)
            (own,) = call(diag_kernel, [shape], state, dblock, macs=dblock.size)
            state, _ = call(
                sweep_kernel, [shape, shape], state, others, own, resid, dblock, lblocks, cols,
                macs=dblock.size + lblocks.size,
            )
        return state

    def apply(vec):
        others = gathered(vec, count)
        near_parts = [lax.ppermute(vec, "sub", swap(subs, 1 << bit)) for bit in range(3)]
        (own,) = call(diag_kernel, [shape], vec, dblock, macs=dblock.size)
        (known,) = call(off_kernel, [shape], vec, others, own, lblocks, cols, macs=lblocks.size)
        return [known, *near_parts, fblock]

    state, message, _ = call(
        first_kernel, [shape, parcel, scratch], resid, dblock, zvec, macs=dblock.size + zvec.size
    )
    arrived = everywhere(message)
    state = smooth(resid, state)
    (first,) = call(
        functools.partial(direction_kernel, count), [shape], state, arrived, inverse, zvec, macs=zvec.size
    )
    image, state, message, _ = call(
        image_kernel, [shape, shape, parcel, scratch], *apply(first), resid, dblock, zvec,
        macs=dblock.size + zvec.size + fblock.size,
    )
    arrived = everywhere(message)
    state = smooth(image, state)
    second, rest, alpha = call(
        functools.partial(next_direction_kernel, count), [shape, shape, (8, shape[1])],
        state, arrived, inverse, zvec, first, resid, image, macs=zvec.size,
    )
    image, message = call(last_image_kernel, [shape, parcel], *apply(second), rest, macs=fblock.size)
    arrived = everywhere(message)
    field, rest = call(final_kernel, [shape, shape], arrived, alpha, first, second, rest, image)
    return field[None], rest[None]


def solution(mesh):
    placed = (
        P("sub", None, "coarse"),
        P("sub", None, None, None, "coarse"),
        P("sub", None, None, "coarse"),
        P("sub", None, None, "coarse"),
        P("sub", None, "coarse"),
        P("sub", None, None, "coarse"),
        P("sub", None),
    )
    return jax.shard_map(
        functools.partial(local, mesh.shape["sub"], mesh.shape["coarse"]),
        mesh=mesh,
        in_specs=placed,
        out_specs=(P("sub", None, "coarse"), P("sub", None, "coarse")),
        check_vma=False,
    )
```

```python
import functools

import jax
import jax.numpy as jnp
from jax import lax
from jax.experimental import pallas as pl
from jax.experimental.pallas import tpu as pltpu
from jax.sharding import PartitionSpec as P

SWEEPS = 3
ITERS = 2
ROWS = 8
SCOPED = 2 << 20
HIGH = lax.Precision.HIGHEST


def in_vmem(array):
    return pltpu.with_memory_space_constraint(array, pltpu.VMEM)


def kernel(body, outs, args, scratch=(), **kwargs):
    return pl.pallas_call(
        body,
        out_shape=outs,
        scratch_shapes=[pltpu.VMEM(shape, jnp.float32) if isinstance(shape, tuple) else shape for shape in scratch],
        cost_estimate=pl.CostEstimate(flops=0, bytes_accessed=0, transcendentals=0),
        compiler_params=pltpu.CompilerParams(vmem_limit_bytes=SCOPED),
        **kwargs,
    )(*args)


def call(body, outs, *args, keep=(), scratch=()):
    count = len(args)
    args = [in_vmem(a) for a in (*args, *keep)]

    def inner(*refs):
        body(*refs[:count], *refs[len(args) :])

    return kernel(
        inner,
        [pltpu.VMEM(shape, jnp.float32) for shape in outs],
        args,
        scratch,
        in_specs=[pl.BlockSpec(memory_space=pltpu.VMEM) for _ in args],
        out_specs=[pl.BlockSpec(memory_space=pltpu.VMEM) for _ in outs],
    )


def rows_times(blocks, vec, start):
    chunk = blocks[pl.ds(start, ROWS)].astype(jnp.float32)
    return jnp.sum(chunk * vec[None], axis=1)


def by_rows(count, body):
    def step(at, carry):
        body(pl.multiple_of(at * ROWS, ROWS))
        return carry

    lax.fori_loop(0, count // ROWS, step, 0)


def block_product(blocks, vec, out):
    def body(start):
        out[pl.ds(start, ROWS), :] = rows_times(blocks, vec, start)

    by_rows(blocks.shape[0], body)


def relaxed(dblock, vec, out, base=None):
    def body(start):
        part = dblock_rows(dblock, vec, start)
        value = part if base is None else base[pl.ds(start, ROWS), :] + part
        out[pl.ds(start, ROWS), :] = value

    whole = vec[...]

    def dblock_rows(blocks, ref, start):
        return 0.25 * (2.0 * ref[pl.ds(start, ROWS), :] - 0.25 * rows_times(blocks, whole, start))

    by_rows(dblock.shape[0], body)


def restricted(zvec, vec, scratch):
    block_product(zvec, vec, scratch)
    nvec, lanes = scratch.shape
    stacked = jnp.concatenate([scratch[...]] * (lanes // nvec), axis=0)
    ones = jnp.ones((ROWS, lanes), jnp.float32)
    return lax.dot_general(
        ones, stacked, (((1,), (1,)), ((), ())), precision=HIGH, preferred_element_type=jnp.float32
    )


def post(message, nvec, sums, cross, square):
    sub = lax.axis_index("sub")
    lane = lax.broadcasted_iota(jnp.int32, (ROWS, message.shape[-1]), 1)
    groups = message.shape[-1] // nvec
    group, place = lane // nvec, lax.rem(lane, nvec)
    pair = jnp.where(place == 0, cross, jnp.where(place == 1, square, 0.0))
    row = jnp.where(group == lax.rem(sub + 1, groups), pair, 0.0)
    row = jnp.where(group == lax.rem(sub, groups), sums, row)
    if len(message.shape) == 3:
        message[...] = jnp.broadcast_to(row[None], message.shape)
    else:
        for at in range(message.shape[0] // ROWS):
            message[at * ROWS : (at + 1) * ROWS, :] = row


def total(x):
    return jnp.sum(x, keepdims=True)


def brought(sources, targets, done):
    copies = [
        pltpu.make_async_copy(source, target, done.at[at])
        for at, (source, target) in enumerate(zip(sources, targets))
    ]
    for copy in copies:
        copy.start()
    return copies


def first_kernel(resid_far, zvec_far, resid, message, zvec, scratch, done):
    for copy in brought((resid_far, zvec_far), (resid, zvec), done):
        copy.wait()
    zero = jnp.zeros((ROWS, message.shape[-1]), jnp.float32)
    post(message, zvec.shape[0], restricted(zvec, resid[...], scratch), zero, zero)


def second_kernel(*refs):
    resid, count = refs[0], (len(refs) - 4) // 2
    sources, targets = refs[1 : 1 + count], refs[1 + count : 1 + 2 * count]
    state, own, done = refs[1 + 2 * count :]
    copies = brought(sources, targets, done)
    copies[0].wait()
    relaxed(targets[0], resid, state)
    block_product(targets[0], state[...], own)
    for copy in copies[1:]:
        copy.wait()


def diag_kernel(vec, dblock, out):
    block_product(dblock, vec[...], out)


def picked(vec, others, cols, part):
    me = lax.axis_index("coarse")
    width = vec.shape[1]
    index = jnp.broadcast_to(cols[pl.ds(part, 1), :], vec.shape)
    owner = index // width
    place = lax.rem(index, width)

    def lanes(block):
        return jnp.take_along_axis(block, place, axis=1, mode="promise_in_bounds")

    if others.shape[0] == 1:
        return jnp.where(owner == me, lanes(vec[...]), lanes(others[0]))
    value = lanes(others[0])
    for at in range(1, others.shape[0]):
        value = jnp.where(owner == at, lanes(others[at]), value)
    return value


def off_rows(lblocks, chosen, start):
    value = rows_times(lblocks.at[0], chosen[0], start)
    for part in range(1, len(chosen)):
        value = value + rows_times(lblocks.at[part], chosen[part], start)
    return value


def sweep_kernel(state, others, own, resid, dblock, lblocks, cols, out, rest):
    chosen = [picked(state, others, cols, part) for part in range(lblocks.shape[0])]

    def body(start):
        here = pl.ds(start, ROWS)
        rest[here, :] = resid[here, :] - (own[here, :] + off_rows(lblocks, chosen, start))

    by_rows(dblock.shape[0], body)
    relaxed(dblock, rest, out, state)


def off_kernel(vec, others, own, lblocks, cols, out):
    chosen = [picked(vec, others, cols, part) for part in range(lblocks.shape[0])]

    def body(start):
        out[pl.ds(start, ROWS), :] = own[pl.ds(start, ROWS), :] + off_rows(lblocks, chosen, start)

    by_rows(out.shape[0], body)


def step_size(arrived, nvec, count):
    lane = lax.broadcasted_iota(jnp.int32, arrived.shape, 1)
    sender = lax.broadcasted_iota(jnp.int32, arrived.shape, 0)
    groups = arrived.shape[1] // nvec
    values = jnp.where(lane // nvec == lax.rem(sender // count + 1, groups), arrived[...], 0.0)
    place = lax.rem(lane, nvec)
    cross = total(jnp.where(place == 0, values, 0.0))
    square = total(jnp.where(place == 1, values, 0.0))
    return cross / (square + 1e-06)


def corrected(state, arrived, inverse, zvec, count):
    nvec, lanes = zvec.shape[0], state.shape[1]
    groups = lanes // nvec
    each = count * groups
    lane = lax.broadcasted_iota(jnp.int32, (each, lanes), 1)
    sender = lax.broadcasted_iota(jnp.int32, (each, lanes), 0)
    keep = lane // nvec == sender // count
    acc = jnp.zeros((nvec, lanes), jnp.float32)
    for at in range(inverse.shape[1] // lanes):
        row = jnp.where(keep, arrived[at * each : (at + 1) * each, :], 0.0)
        acc = acc + inverse[:, at * lanes : (at + 1) * lanes] * jnp.sum(row, axis=0, keepdims=True)
    weights = jnp.broadcast_to(jnp.sum(acc, axis=1, keepdims=True), acc.shape)
    value = state[...]
    for at in range(nvec):
        value = value + weights[at : at + 1, :] * zvec[at].astype(jnp.float32)
    return value


def direction_kernel(count, state, arrived, inverse, zvec, out):
    out[...] = corrected(state, arrived, inverse, zvec, count)


def next_direction_kernel(count, state, arrived, inverse, zvec, previous, resid, image, out, rest, alpha):
    size = step_size(arrived, zvec.shape[0], count)
    out[...] = previous[...] - size * corrected(state, arrived, inverse, zvec, count)
    rest[...] = resid[...] - size * image[...]
    alpha[...] = jnp.broadcast_to(size, alpha.shape)


def near(parts, inner):
    lane = lax.broadcasted_iota(jnp.int32, parts[0].shape, 1)
    value = parts[0][...]
    for at in range(1, len(parts)):
        value = jnp.where(lane < at * inner, value, parts[at][...])
    return value[:, : len(parts) * inner]


def with_interface(known, parts, fblock, out):
    width = fblock.shape[2]
    vec = near(parts, width // len(parts))

    def body(start):
        here = pl.ds(start, ROWS)
        add = rows_times(fblock, vec, start)
        pad = jnp.zeros((ROWS, out.shape[1] - width), jnp.float32)
        out[here, :] = known[here, :] + jnp.concatenate([add, pad], axis=1)

    by_rows(out.shape[0], body)


def image_kernel(known, near0, near1, near2, fblock, resid, dblock, zvec, image, state, own, message, scratch):
    with_interface(known, (near0, near1, near2), fblock, image)
    value = image[...]
    sums = restricted(zvec, value, scratch)
    post(message, zvec.shape[0], sums, total(resid[...] * value), total(value * value))
    relaxed(dblock, image, state)
    block_product(dblock, state[...], own)


def last_image_kernel(nvec, known, near0, near1, near2, fblock, resid, image, message):
    with_interface(known, (near0, near1, near2), fblock, image)
    value = image[...]
    zero = jnp.zeros((ROWS, message.shape[-1]), jnp.float32)
    post(message, nvec, zero, total(resid[...] * value), total(value * value))


def final_kernel(nvec, count, arrived, alpha, first, second, resid, image, field, rest):
    size = step_size(arrived, nvec, count)
    field[0] = alpha[0:1, :] * first[...] + size * second[...]
    rest[0] = resid[...] - size * image[...]


def swap(count, apart):
    return [(low, low ^ apart) for low in range(count) if low ^ apart < count]


def gathered(vec, count):
    if count == 2:
        return lax.ppermute(vec, "coarse", swap(2, 1))[None]
    return lax.all_gather(vec, "coarse", axis=0)


def local(subs, count, right_side, local_blocks, diag_blocks, iface_blocks, block_cols, basis, coarse_inverse):
    shape = right_side.shape[1:]
    nvec = basis.shape[1]
    parcel = (subs * count, shape[1])
    wide = (subs * count, ROWS, shape[1])

    def everywhere(message):
        return lax.all_to_all(message, ("sub", "coarse"), 0, 0, tiled=True)

    def smooth(resid, state, own):
        for sweep in range(SWEEPS - 1):
            others = gathered(state, count)
            if sweep:
                (own,) = call(diag_kernel, [shape], state, dblock, keep=held)
            (state,) = call(
                sweep_kernel, [shape], state, others, own, resid, dblock, lblocks, cols,
                keep=held, scratch=[shape],
            )
        return state

    def apply(vec):
        others = gathered(vec, count)
        near_parts = [lax.ppermute(vec, "sub", swap(subs, 1 << bit)) for bit in range(3)]
        (own,) = call(diag_kernel, [shape], vec, dblock, keep=held)
        (known,) = call(off_kernel, [shape], vec, others, own, lblocks, cols, keep=held)
        return [known, *near_parts, fblock]

    def far(array):
        return pltpu.with_memory_space_constraint(array, pltpu.HBM)

    def near_to(*shapes):
        return [pl.BlockSpec(memory_space=pltpu.VMEM) for _ in shapes]

    zvec, fblock = basis[0], iface_blocks[0]
    outs = [pltpu.VMEM(s, jnp.float32) for s in (shape, wide)]
    resid, message = kernel(
        first_kernel,
        outs,
        [far(right_side[0]), far(zvec)],
        [pltpu.VMEM(zvec.shape, zvec.dtype), (nvec, shape[1]), pltpu.SemaphoreType.DMA((2,))],
        in_specs=[pl.BlockSpec(memory_space=pl.ANY)] * 2,
        out_specs=near_to(*outs),
    )
    arrived = everywhere(message)[:, 0, :]
    sources = [diag_blocks[0], local_blocks[0], block_cols[0], coarse_inverse]
    outs = [pltpu.VMEM(a.shape, a.dtype) for a in sources] + [pltpu.VMEM(shape, jnp.float32)] * 2
    *held, state, own = kernel(
        second_kernel,
        outs,
        [in_vmem(resid), *map(far, sources)],
        [pltpu.SemaphoreType.DMA((len(sources),))],
        in_specs=[pl.BlockSpec(memory_space=pltpu.VMEM)] + [pl.BlockSpec(memory_space=pl.ANY)] * len(sources),
        out_specs=near_to(*outs),
    )
    dblock, lblocks, cols, inverse = held
    held = ()
    state = smooth(resid, state, own)
    (first,) = call(
        functools.partial(direction_kernel, count), [shape], state, arrived, inverse, zvec, keep=held,
    )
    image, state, own, message = call(
        image_kernel, [shape, shape, shape, wide], *apply(first), resid, dblock, zvec,
        keep=held, scratch=[(nvec, shape[1])],
    )
    arrived = everywhere(message)[:, 0, :]
    state = smooth(image, state, own)
    second, rest, alpha = call(
        functools.partial(next_direction_kernel, count), [shape, shape, (ROWS, shape[1])],
        state, arrived, inverse, zvec, first, resid, image, keep=held,
    )
    image, message = call(
        functools.partial(last_image_kernel, nvec), [shape, parcel], *apply(second), rest,
    )
    arrived = everywhere(message)
    operands = [in_vmem(a) for a in (arrived, alpha, first, second, rest, image)]
    return kernel(
        functools.partial(final_kernel, nvec, count),
        [jax.ShapeDtypeStruct((1, *shape), jnp.float32)] * 2,
        operands,
        in_specs=[pl.BlockSpec(memory_space=pltpu.VMEM) for _ in operands],
    )


def solution(mesh):
    placed = (
        P("sub", None, "coarse"),
        P("sub", None, None, None, "coarse"),
        P("sub", None, None, "coarse"),
        P("sub", None, None, "coarse"),
        P("sub", None, "coarse"),
        P("sub", None, None, "coarse"),
        P("sub", None),
    )
    return jax.shard_map(
        functools.partial(local, mesh.shape["sub"], mesh.shape["coarse"]),
        mesh=mesh,
        in_specs=placed,
        out_specs=(P("sub", None, "coarse"), P("sub", None, "coarse")),
        check_vma=False,
    )
```

```python
import functools

import jax
import jax.numpy as jnp
from jax import lax
from jax.experimental import pallas as pl
from jax.experimental.pallas import tpu as pltpu
from jax.sharding import PartitionSpec as P

SWEEPS = 3
ITERS = 2
BITS = 3
ROWS = 8
WIDE = 3
SCOPED = 6 << 20
HIGH = lax.Precision.HIGHEST


def kernel(body, outs, near, far=(), scratch=()):
    near = [pltpu.with_memory_space_constraint(a, pltpu.VMEM) for a in near]
    far = [pltpu.with_memory_space_constraint(a, pltpu.HBM) for a in far]
    there, here = pl.BlockSpec(memory_space=pl.ANY), pl.BlockSpec(memory_space=pltpu.VMEM)
    return pl.pallas_call(
        body,
        out_shape=outs,
        in_specs=[here] * len(near) + [there] * len(far),
        out_specs=[there if o.memory_space == pltpu.HBM else here for o in outs],
        scratch_shapes=scratch,
        cost_estimate=pl.CostEstimate(flops=0, bytes_accessed=0, transcendentals=0),
        compiler_params=pltpu.CompilerParams(vmem_limit_bytes=SCOPED),
    )(*near, *far)


def vmem(shape, dtype=jnp.float32):
    return pltpu.VMEM(tuple(shape), dtype)


def start_all(sources, targets, done, first=0):
    copies = [
        pltpu.make_async_copy(source, target, done.at[first + at])
        for at, (source, target) in enumerate(zip(sources, targets))
    ]
    for copy in copies:
        copy.start()
    return copies


def wait_all(copies):
    for copy in copies:
        copy.wait()


def by_rows(count, body, step=ROWS):
    def turn(at, carry):
        body(pl.multiple_of(at * step, step))
        return carry

    lax.fori_loop(0, count // step, turn, 0)


def rows_times(blocks, vec, start):
    chunk = blocks[pl.ds(start, ROWS)].astype(jnp.float32)
    return jnp.sum(chunk * vec[None], axis=1)


def block_product(blocks, vec, out):
    def body(start):
        out[pl.ds(start, ROWS), :] = rows_times(blocks, vec, start)

    by_rows(blocks.shape[0], body)


def relaxed(dblock, vec, out, base=None):
    whole = vec[...]

    def body(start):
        here = pl.ds(start, ROWS)
        part = 0.25 * (2.0 * vec[here, :] - 0.25 * rows_times(dblock, whole, start))
        out[here, :] = part if base is None else base[here, :] + part

    by_rows(dblock.shape[0], body)


def restricted(zvec, vec, scratch):
    block_product(zvec, vec, scratch)
    sums = jnp.broadcast_to(jnp.sum(scratch[...], axis=1, keepdims=True), scratch.shape)
    lane = lax.broadcasted_iota(jnp.int32, sums.shape, 1)
    row = lax.broadcasted_iota(jnp.int32, sums.shape, 0)
    return jnp.sum(jnp.where(lax.rem(lane, sums.shape[0]) == row, sums, 0.0), axis=0, keepdims=True)


def post(message, nvec, sums, cross, square):
    sub = lax.axis_index("sub")
    lanes = message.shape[-1]
    lane = lax.broadcasted_iota(jnp.int32, (ROWS, lanes), 1)
    groups = lanes // nvec
    group, place = lane // nvec, lax.rem(lane, nvec)
    pair = jnp.where(place == 0, cross, jnp.where(place == 1, square, 0.0))
    row = jnp.where(group == lax.rem(sub + 1, groups), pair, 0.0)
    row = jnp.where(group == lax.rem(sub, groups), sums, row)
    if len(message.shape) == 3:
        message[...] = jnp.broadcast_to(row[None, : message.shape[1]], message.shape)
    else:
        for at in range(message.shape[0] // ROWS):
            message[at * ROWS : (at + 1) * ROWS, :] = row


def total(x):
    return jnp.sum(x, keepdims=True)


def step_size(arrived, nvec, count):
    lane = lax.broadcasted_iota(jnp.int32, arrived.shape, 1)
    sender = lax.broadcasted_iota(jnp.int32, arrived.shape, 0)
    groups = arrived.shape[1] // nvec
    values = jnp.where(lane // nvec == lax.rem(sender // count + 1, groups), arrived[...], 0.0)
    place = lax.rem(lane, nvec)
    cross = total(jnp.where(place == 0, values, 0.0))
    square = total(jnp.where(place == 1, values, 0.0))
    return cross / (square + 1e-06)


def restriction_rows(arrived, nvec, count):
    lanes = arrived.shape[1]
    each = count * (lanes // nvec)
    lane = lax.broadcasted_iota(jnp.int32, (each, lanes), 1)
    sender = lax.broadcasted_iota(jnp.int32, (each, lanes), 0)
    keep = lane // nvec == sender // count
    return [
        jnp.sum(jnp.where(keep, arrived[at : at + each, :], 0.0), axis=0, keepdims=True)
        for at in range(0, arrived.shape[0], each)
    ]


def weights_here(inverse, rows):
    lanes = rows[0].shape[1]
    acc = inverse[:, :lanes] * rows[0]
    for at in range(1, len(rows)):
        acc = acc + inverse[:, at * lanes : (at + 1) * lanes] * rows[at]
    return jnp.broadcast_to(jnp.sum(acc, axis=1, keepdims=True), acc.shape)


def combined(weights, zvec, value):
    for at in range(weights.shape[0]):
        value = value + weights[at : at + 1, :] * zvec[at].astype(jnp.float32)
    return value


def picked(vec, others, cols, part):
    me = lax.axis_index("coarse")
    width = vec.shape[1]
    index = jnp.broadcast_to(cols[pl.ds(part, 1), :], vec.shape)
    owner = index // width
    place = lax.rem(index, width)

    def lanes(block):
        return jnp.take_along_axis(block, place, axis=1, mode="promise_in_bounds")

    if others.shape[0] == 1:
        return jnp.where(owner == me, lanes(vec[...]), lanes(others[0]))
    value = lanes(others[0])
    for at in range(1, others.shape[0]):
        value = jnp.where(owner == at, lanes(others[at]), value)
    return value


def off_rows(lblocks, chosen, start):
    value = rows_times(lblocks.at[0], chosen[0], start)
    for part in range(1, len(chosen)):
        value = value + rows_times(lblocks.at[part], chosen[part], start)
    return value


def with_interface(known, vec, fblock, out):
    width = fblock.shape[2]
    vec = vec[:, :width]

    def body(start):
        here = pl.ds(start, ROWS)
        add = rows_times(fblock, vec, start)
        pad = jnp.zeros((ROWS, out.shape[1] - width), jnp.float32)
        out[here, :] = known[here, :] + jnp.concatenate([add, pad], axis=1)

    by_rows(out.shape[0], body)


def first_kernel(resid_far, zvec_far, dblock_far, resid, dblock, message_far, zvec, scratch, message, done):
    copies = start_all((resid_far, zvec_far, dblock_far), (resid, zvec, dblock), done)
    wait_all(copies[:2])
    zero = jnp.zeros((1, message.shape[-1]), jnp.float32)
    post(message, zvec.shape[0], restricted(zvec, resid[...], scratch), zero, zero)
    wait_all(copies[2:] + start_all((message,), (message_far,), done, 3))


def relax_kernel(vec, dblock, out):
    relaxed(dblock, vec, out)


def diag_kernel(vec, dblock, *refs):
    count = (len(refs) - 2) // 2
    copies = start_all(refs[:count], refs[count + 1 : -1], refs[-1])
    block_product(dblock, vec[...], refs[count])
    wait_all(copies)


def diag_from_far_kernel(vec, dblock_far, out, dblock, done):
    wait_all(start_all((dblock_far,), (dblock,), done))
    block_product(dblock, vec[...], out)


def apply_kernel(diag_near, vec, others, cols, here, there, fblock_far, out, fblock, arrived, done):
    copies = start_all((there, fblock_far), (arrived, fblock), done)
    dblock, lblocks = (here, arrived) if diag_near else (arrived, here)
    chosen = [picked(vec, others, cols, part) for part in range(lblocks.shape[0])]
    whole = vec[...]

    def own(start):
        return rows_times(dblock, whole, start)

    def off(start):
        return off_rows(lblocks, chosen, start)

    first, second = (own, off) if diag_near else (off, own)

    def begin(start):
        out[pl.ds(start, ROWS), :] = first(start)

    def finish(start):
        rows = pl.ds(start, ROWS)
        out[rows, :] = out[rows, :] + second(start)

    by_rows(out.shape[0], begin)
    copies[0].wait()
    by_rows(out.shape[0], finish)
    copies[1].wait()


def sweep_kernel(state, others, own, resid, dblock, lblocks, cols, out, rest):
    chosen = [picked(state, others, cols, part) for part in range(lblocks.shape[0])]

    def body(start):
        here = pl.ds(start, ROWS)
        rest[here, :] = resid[here, :] - (own[here, :] + off_rows(lblocks, chosen, start))

    by_rows(dblock.shape[0], body)
    relaxed(dblock, rest, out, state)


def direction_kernel(count, state, arrived, zvec, inverse, out):
    rows = restriction_rows(arrived, zvec.shape[0], count)
    out[...] = combined(weights_here(inverse, rows), zvec, state[...])


def near_lanes(parts, inner):
    group = lax.broadcasted_iota(jnp.int32, parts[0].shape, 1) // inner
    value = parts[0][...]
    for at in range(1, len(parts)):
        value = jnp.where(group == at, parts[at][...], value)
    return value


def image_kernel(known, near0, near1, near2, fblock, resid, zvec, dblock, image, state, message_far, scratch, message, done):
    with_interface(known, near_lanes((near0, near1, near2), fblock.shape[2] // BITS), fblock, image)
    value = image[...]
    sums = restricted(zvec, value, scratch)
    post(message, zvec.shape[0], sums, total(resid[...] * value), total(value * value))
    copies = start_all((message,), (message_far,), done)
    relaxed(dblock, image, state)
    wait_all(copies)


def next_direction_kernel(count, state, arrived, zvec, inverse, first, resid, image, out, rest, alpha):
    size = step_size(arrived, zvec.shape[0], count)
    rows = restriction_rows(arrived, zvec.shape[0], count)
    out[...] = first[...] - size * combined(weights_here(inverse, rows), zvec, state[...])
    rest[...] = resid[...] - size * image[...]
    alpha[...] = jnp.broadcast_to(size, alpha.shape)


def last_image_kernel(nvec, known, near0, near1, near2, fblock, resid, image, message):
    with_interface(known, near_lanes((near0, near1, near2), fblock.shape[2] // BITS), fblock, image)
    value = image[...]
    zero = jnp.zeros((1, message.shape[-1]), jnp.float32)
    post(message, nvec, zero, total(resid[...] * value), total(value * value))


def final_kernel(nvec, count, arrived, alpha, first, second, resid, image, field, rest):
    size = step_size(arrived, nvec, count)
    field[0] = alpha[0:1, :] * first[...] + size * second[...]
    rest[0] = resid[...] - size * image[...]


def swap(count, apart):
    return [(low, low ^ apart) for low in range(count) if low ^ apart < count]


def gathered(array, count):
    if count == 2:
        return lax.ppermute(array, "coarse", swap(2, 1))[None]
    return lax.all_gather(array, "coarse", axis=0)


def local(subs, count, right_side, local_blocks, diag_blocks, iface_blocks, block_cols, basis, coarse_inverse):
    lfar, dfar, ffar = local_blocks[0], diag_blocks[0], iface_blocks[0]
    cfar, zfar = block_cols[0], basis[0]
    shape = right_side.shape[1:]
    nvec, lanes = zfar.shape[0], shape[1]
    flat, small, parcel = vmem(shape), vmem((nvec, lanes)), vmem((subs * count, lanes))
    wide = vmem((subs * count, WIDE, lanes))

    def sems(number):
        return pltpu.SemaphoreType.DMA((number,))

    def like(array, space=vmem):
        return space(array.shape, array.dtype)

    def everywhere(message):
        return lax.all_to_all(message, ("sub", "coarse"), 0, 0, tiled=len(message.shape) == 2)

    def sweep(state, others, own, resid, dblock, lblocks, cols):
        (out,) = kernel(sweep_kernel, [flat], [state, others, own, resid, dblock, lblocks, cols], (), [flat])
        return out

    def diag(vec, dblock, *far):
        return kernel(diag_kernel, [flat, *map(like, far)], [vec, dblock], far, [sems(max(len(far), 1))])

    def middle(state, resid, dblock, lblocks, cols):
        for _ in range(SWEEPS - 3):
            others = gathered(state, count)
            (own,) = diag(state, dblock)
            state = sweep(state, others, own, resid, dblock, lblocks, cols)
        return state

    def last_sweep(state, resid, dblock, lblocks, cols):
        others = gathered(state, count)
        own, *held = diag(state, dblock, zfar, coarse_inverse)
        return sweep(state, others, own, resid, dblock, lblocks, cols), held

    def apply(vec, cols, here, there, last=False):
        others = gathered(vec, count)
        near = [lax.ppermute(vec, "sub", swap(subs, 1 << bit)) for bit in range(BITS)]
        outs, scratch = [flat, like(ffar)], [like(there)]
        if not last:
            outs, scratch = outs + scratch, []
        known, fblock, *brought = kernel(
            functools.partial(apply_kernel, len(here.shape) < len(there.shape)),
            outs,
            [vec, others, cols, here],
            [there, ffar],
            [*scratch, sems(2)],
        )
        return [known, *near, fblock], brought

    wide_far = pltpu.HBM(wide.shape, jnp.float32)
    resid, dblock, message = kernel(
        first_kernel,
        [flat, like(dfar), wide_far],
        [],
        [right_side[0], zfar, dfar],
        [like(zfar), small, wide, sems(4)],
    )
    arrived = everywhere(message)[:, 0, :]
    (state,) = kernel(relax_kernel, [flat], [resid, dblock])
    others = gathered(state, count)
    own, lblocks, cols = diag(state, dblock, lfar, cfar)
    state = sweep(state, others, own, resid, dblock, lblocks, cols)
    state = middle(state, resid, dblock, lblocks, cols)
    state, held = last_sweep(state, resid, dblock, lblocks, cols)
    (first,) = kernel(functools.partial(direction_kernel, count), [flat], [state, arrived, *held])
    terms, (lblocks,) = apply(first, cols, dblock, lfar)
    first_image, state, message = kernel(
        image_kernel, [flat, flat, wide_far], [*terms, resid, held[0], dblock], [], [small, wide, sems(1)]
    )
    arrived = everywhere(message)[:, 0, :]
    others = gathered(state, count)
    own, dblock = kernel(diag_from_far_kernel, [flat, like(dfar)], [state], [dfar], [sems(1)])
    state = sweep(state, others, own, first_image, dblock, lblocks, cols)
    state = middle(state, first_image, dblock, lblocks, cols)
    state, held = last_sweep(state, first_image, dblock, lblocks, cols)
    second, rest, alpha = kernel(
        functools.partial(next_direction_kernel, count),
        [flat, flat, vmem((ROWS, lanes))],
        [state, arrived, *held, first, resid, first_image],
    )
    terms, _ = apply(second, cols, lblocks, dfar, True)
    image, message = kernel(functools.partial(last_image_kernel, nvec), [flat, parcel], [*terms, rest])
    arrived = everywhere(message)
    return pl.pallas_call(
        functools.partial(final_kernel, nvec, count),
        out_shape=[jax.ShapeDtypeStruct((1, *shape), jnp.float32)] * 2,
        in_specs=[pl.BlockSpec(memory_space=pltpu.VMEM)] * 6,
        compiler_params=pltpu.CompilerParams(vmem_limit_bytes=SCOPED),
    )(*[pltpu.with_memory_space_constraint(a, pltpu.VMEM) for a in (arrived, alpha, first, second, rest, image)])


def solution(mesh):
    placed = (
        P("sub", None, "coarse"),
        P("sub", None, None, None, "coarse"),
        P("sub", None, None, "coarse"),
        P("sub", None, None, "coarse"),
        P("sub", None, "coarse"),
        P("sub", None, None, "coarse"),
        P("sub", None),
    )
    return jax.shard_map(
        functools.partial(local, mesh.shape["sub"], mesh.shape["coarse"]),
        mesh=mesh,
        in_specs=placed,
        out_specs=(P("sub", None, "coarse"), P("sub", None, "coarse")),
        check_vma=False,
    )
```

```python
import functools

import jax
import jax.numpy as jnp
from jax import lax
from jax.experimental import pallas as pl
from jax.experimental.pallas import tpu as pltpu
from jax.sharding import PartitionSpec as P

SWEEPS = 3
ITERS = 2
BITS = 3
ROWS = 8
WIDE = 3
SCOPED = 6 << 20
HIGH = lax.Precision.HIGHEST


def kernel(body, outs, near, far=(), scratch=()):
    near = [pltpu.with_memory_space_constraint(a, pltpu.VMEM) for a in near]
    far = [pltpu.with_memory_space_constraint(a, pltpu.HBM) for a in far]
    there, here = pl.BlockSpec(memory_space=pl.ANY), pl.BlockSpec(memory_space=pltpu.VMEM)
    return pl.pallas_call(
        body,
        out_shape=outs,
        in_specs=[here] * len(near) + [there] * len(far),
        out_specs=[there if o.memory_space == pltpu.HBM else here for o in outs],
        scratch_shapes=scratch,
        cost_estimate=pl.CostEstimate(flops=0, bytes_accessed=0, transcendentals=0),
        compiler_params=pltpu.CompilerParams(vmem_limit_bytes=SCOPED),
    )(*near, *far)


def vmem(shape, dtype=jnp.float32):
    return pltpu.VMEM(tuple(shape), dtype)


def start_all(sources, targets, done, first=0):
    copies = [
        pltpu.make_async_copy(source, target, done.at[first + at])
        for at, (source, target) in enumerate(zip(sources, targets))
    ]
    for copy in copies:
        copy.start()
    return copies


def wait_all(copies):
    for copy in copies:
        copy.wait()


def by_rows(count, body, step=ROWS):
    for start in range(0, count, step):
        body(start)


def rows_times(blocks, vec, start):
    chunk = blocks[pl.ds(start, ROWS)].astype(jnp.float32)
    return jnp.sum(chunk * vec[None], axis=1)


def block_product(blocks, vec, out):
    def body(start):
        out[pl.ds(start, ROWS), :] = rows_times(blocks, vec, start)

    by_rows(blocks.shape[0], body)


def relaxed(dblock, vec, out, base=None):
    whole = vec[...]

    def body(start):
        here = pl.ds(start, ROWS)
        part = 0.25 * (2.0 * vec[here, :] - 0.25 * rows_times(dblock, whole, start))
        out[here, :] = part if base is None else base[here, :] + part

    by_rows(dblock.shape[0], body)


def dot_rows(left, right):
    return jnp.sum(left * right, axis=0, keepdims=True)


def post(message, scratch):
    sub = lax.axis_index("sub")
    lanes = scratch.shape[1]
    nvec = scratch.shape[0] - ROWS
    groups = lanes // nvec
    sums = jnp.broadcast_to(jnp.sum(scratch[...], axis=1, keepdims=True), scratch.shape)
    lane = lax.broadcasted_iota(jnp.int32, scratch.shape, 1)
    row = lax.broadcasted_iota(jnp.int32, scratch.shape, 0)
    place = lax.rem(sub + row // nvec, groups) * nvec + lax.rem(row, nvec)
    line = jnp.sum(jnp.where(lane == place, sums, 0.0), axis=0, keepdims=True)
    if len(message.shape) == 3:
        message[...] = jnp.broadcast_to(line[None], message.shape)
    else:
        message[...] = jnp.broadcast_to(line, message.shape)


def inner_products(scratch, resid, image):
    nvec = scratch.shape[0] - ROWS
    scratch[nvec:, :] = jnp.concatenate(
        [dot_rows(resid, image), dot_rows(image, image), jnp.zeros((ROWS - 2, image.shape[1]), jnp.float32)], axis=0
    )


def total(x):
    return jnp.sum(x, keepdims=True)


def step_size(arrived, nvec, count):
    lane = lax.broadcasted_iota(jnp.int32, arrived.shape, 1)
    sender = lax.broadcasted_iota(jnp.int32, arrived.shape, 0)
    groups = arrived.shape[1] // nvec
    values = jnp.where(lane // nvec == lax.rem(sender // count + 1, groups), arrived[...], 0.0)
    place = lax.rem(lane, nvec)
    cross = total(jnp.where(place == 0, values, 0.0))
    square = total(jnp.where(place == 1, values, 0.0))
    return cross / (square + 1e-06)


def restriction_rows(arrived, nvec, count):
    lanes = arrived.shape[1]
    each = count * (lanes // nvec)
    lane = lax.broadcasted_iota(jnp.int32, (each, lanes), 1)
    sender = lax.broadcasted_iota(jnp.int32, (each, lanes), 0)
    keep = lane // nvec == sender // count
    return [
        jnp.sum(jnp.where(keep, arrived[at : at + each, :], 0.0), axis=0, keepdims=True)
        for at in range(0, arrived.shape[0], each)
    ]


def weights_here(inverse, rows):
    lanes = rows[0].shape[1]
    acc = inverse[:, :lanes] * rows[0]
    for at in range(1, len(rows)):
        acc = acc + inverse[:, at * lanes : (at + 1) * lanes] * rows[at]
    return jnp.broadcast_to(jnp.sum(acc, axis=1, keepdims=True), acc.shape)


def combined(weights, zvec, value):
    for at in range(weights.shape[0]):
        value = value + weights[at : at + 1, :] * zvec[at].astype(jnp.float32)
    return value


def picked(vec, others, cols, part):
    me = lax.axis_index("coarse")
    width = vec.shape[1]
    index = jnp.broadcast_to(cols[pl.ds(part, 1), :], vec.shape)
    owner = index // width
    place = lax.rem(index, width)

    def lanes(block):
        return jnp.take_along_axis(block, place, axis=1, mode="promise_in_bounds")

    if others.shape[0] == 1:
        return jnp.where(owner == me, lanes(vec[...]), lanes(others[0]))
    value = lanes(others[0])
    for at in range(1, others.shape[0]):
        value = jnp.where(owner == at, lanes(others[at]), value)
    return value


def off_rows(lblocks, chosen, start):
    value = rows_times(lblocks.at[0], chosen[0], start)
    for part in range(1, len(chosen)):
        value = value + rows_times(lblocks.at[part], chosen[part], start)
    return value


def with_interface(known, vec, fblock, out):
    width = fblock.shape[2]
    vec = vec[:, :width]

    def body(start):
        here = pl.ds(start, ROWS)
        add = rows_times(fblock, vec, start)
        pad = jnp.zeros((ROWS, out.shape[1] - width), jnp.float32)
        out[here, :] = known[here, :] + jnp.concatenate([add, pad], axis=1)

    by_rows(out.shape[0], body)


def first_kernel(resid_far, zvec_far, dblock_far, resid, dblock, state, message_far, zvec, scratch, message, done):
    pieces = [pl.ds(at, ROWS) for at in range(0, zvec.shape[0], ROWS)]
    copies = start_all(
        [resid_far, *[zvec_far.at[piece] for piece in pieces], dblock_far],
        [resid, *[zvec.at[piece] for piece in pieces], dblock],
        done,
    )
    copies[0].wait()
    vec = resid[...]
    for copy, piece in zip(copies[1:-1], pieces):
        copy.wait()
        scratch[piece, :] = rows_times(zvec, vec, piece.start)
    scratch[zvec.shape[0] :, :] = jnp.zeros((ROWS, vec.shape[1]), jnp.float32)
    post(message, scratch)
    sent = start_all((message,), (message_far,), done, len(copies))
    copies[-1].wait()
    relaxed(dblock, resid, state)
    wait_all(sent)


def diag_kernel(vec, dblock, *refs):
    count = (len(refs) - 2) // 2
    copies = start_all(refs[:count], refs[count + 1 : -1], refs[-1])
    block_product(dblock, vec[...], refs[count])
    wait_all(copies)


def diag_copy_kernel(vec, dblock, *refs):
    count = (len(refs) - 3) // 2
    copies = start_all(refs[:count], refs[count + 2 : -1], refs[-1])
    out, copied = refs[count : count + 2]
    whole = vec[...]

    def body(start):
        rows = pl.ds(start, ROWS)
        out[rows, :] = rows_times(dblock, whole, start)
        copied[rows] = dblock[rows]

    by_rows(out.shape[0], body)
    wait_all(copies)


def apply_kernel(vec, others, cols, lblocks, dblock_far, fblock_far, out, fblock, dblock, done):
    copies = start_all((dblock_far, fblock_far), (dblock, fblock), done)
    chosen = [picked(vec, others, cols, part) for part in range(lblocks.shape[0])]
    whole = vec[...]

    def off(start):
        out[pl.ds(start, ROWS), :] = off_rows(lblocks, chosen, start)

    def own(start):
        rows = pl.ds(start, ROWS)
        out[rows, :] = out[rows, :] + rows_times(dblock, whole, start)

    by_rows(out.shape[0], off)
    copies[0].wait()
    by_rows(out.shape[0], own)
    copies[1].wait()


def sweep_kernel(state, others, own, resid, dblock, lblocks, cols, out, rest):
    chosen = [picked(state, others, cols, part) for part in range(lblocks.shape[0])]

    def body(start):
        here = pl.ds(start, ROWS)
        rest[here, :] = resid[here, :] - (own[here, :] + off_rows(lblocks, chosen, start))

    by_rows(dblock.shape[0], body)
    relaxed(dblock, rest, out, state)


def direction_kernel(count, state, arrived, zvec, inverse, out, *parts):
    rows = restriction_rows(arrived, zvec.shape[0], count)
    value = combined(weights_here(inverse, rows), zvec, state[...])
    out[...] = value
    pack_lanes(value, parts)


def pack_lanes(vec, parts):
    deep, lanes = vec.shape
    rows = parts[0].shape[0]
    groups = deep // rows
    inner = lanes // groups
    group = lax.broadcasted_iota(jnp.int32, (rows, lanes), 1) // inner
    for q, part in enumerate(parts):
        value = jnp.zeros((rows, lanes), jnp.float32)
        for g in range(groups):
            value = jnp.where(group == g, turned(vec[g * rows : (g + 1) * rows, :], (g - q) * inner), value)
        part[...] = value


def turned(value, lanes):
    lanes %= value.shape[1]
    return pltpu.roll(value, lanes, 1) if lanes else value


def near_lanes(parts, deep):
    rows, lanes = parts[0].shape
    groups = deep // rows
    inner = lanes // groups
    group = lax.broadcasted_iota(jnp.int32, (rows, lanes), 1) // inner
    pieces = []
    for g in range(groups):
        value = jnp.zeros((rows, lanes), jnp.float32)
        for q, part in enumerate(parts):
            value = jnp.where(group == q, turned(part[...], (q - g) * inner), value)
        pieces.append(value)
    return jnp.concatenate(pieces, axis=0)


def image_kernel(known, near0, near1, near2, fblock, resid, zvec, dblock, image, state, message_far, scratch, message, done):
    with_interface(known, near_lanes((near0, near1, near2), known.shape[0]), fblock, image)
    value = image[...]
    block_product(zvec, value, scratch)
    inner_products(scratch, resid[...], value)
    post(message, scratch)
    copies = start_all((message,), (message_far,), done)
    relaxed(dblock, image, state)
    wait_all(copies)


def next_direction_kernel(count, state, arrived, zvec, inverse, first, resid, image, out, rest, alpha, *parts):
    size = step_size(arrived, zvec.shape[0], count)
    rows = restriction_rows(arrived, zvec.shape[0], count)
    value = first[...] - size * combined(weights_here(inverse, rows), zvec, state[...])
    out[...] = value
    pack_lanes(value, parts)
    rest[...] = resid[...] - size * image[...]
    alpha[...] = jnp.broadcast_to(size, alpha.shape)


def last_image_kernel(known, near0, near1, near2, fblock, resid, image, message, scratch):
    with_interface(known, near_lanes((near0, near1, near2), known.shape[0]), fblock, image)
    scratch[...] = jnp.zeros(scratch.shape, jnp.float32)
    inner_products(scratch, resid[...], image[...])
    post(message, scratch)


def final_kernel(nvec, count, arrived, alpha, first, second, resid, image, field, rest):
    size = step_size(arrived, nvec, count)
    field[0] = alpha[0:1, :] * first[...] + size * second[...]
    rest[0] = resid[...] - size * image[...]


def swap(count, apart):
    return [(low, low ^ apart) for low in range(count) if low ^ apart < count]


def gathered(array, count):
    if count == 2:
        return lax.ppermute(array, "coarse", swap(2, 1))[None]
    return lax.all_gather(array, "coarse", axis=0)


def local(subs, count, right_side, local_blocks, diag_blocks, iface_blocks, block_cols, basis, coarse_inverse):
    lfar, dfar, ffar = local_blocks[0], diag_blocks[0], iface_blocks[0]
    cfar, zfar = block_cols[0], basis[0]
    shape = right_side.shape[1:]
    nvec, lanes = zfar.shape[0], shape[1]
    flat, small, parcel = vmem(shape), vmem((nvec + ROWS, lanes)), vmem((subs * count, lanes))
    wide = vmem((subs * count, WIDE, lanes))

    def sems(number):
        return pltpu.SemaphoreType.DMA((number,))

    def like(array, space=vmem):
        return space(array.shape, array.dtype)

    def everywhere(message):
        return lax.all_to_all(message, ("sub", "coarse"), 0, 0, tiled=len(message.shape) == 2)

    def sweep(state, others, own, resid, dblock, lblocks, cols):
        (out,) = kernel(sweep_kernel, [flat], [state, others, own, resid, dblock, lblocks, cols], (), [flat])
        return out

    def diag(vec, dblock, *far):
        return kernel(diag_kernel, [flat, *map(like, far)], [vec, dblock], far, [sems(max(len(far), 1))])

    def smooth(state, resid, dblock, lblocks, cols, *far):
        others = gathered(state, count)
        own, dblock, *more = kernel(
            diag_copy_kernel,
            [flat, like(dblock), *map(like, far)],
            [state, dblock],
            far,
            [sems(max(len(far), 1))],
        )
        lblocks, cols = more or (lblocks, cols)
        state = sweep(state, others, own, resid, dblock, lblocks, cols)
        for at in range(SWEEPS - 2):
            others = gathered(state, count)
            own, *held = diag(state, dblock, *((zfar, coarse_inverse) if at == SWEEPS - 3 else ()))
            state = sweep(state, others, own, resid, dblock, lblocks, cols)
        return state, held, lblocks, cols

    def apply(vec, parts, lblocks, cols, last=False):
        others = gathered(vec, count)
        near = [lax.ppermute(part, "sub", swap(subs, 1 << bit)) for bit, part in enumerate(parts)]
        outs, scratch = [flat, like(ffar)], [like(dfar)]
        if not last:
            outs, scratch = outs + scratch, []
        known, fblock, *brought = kernel(
            apply_kernel, outs, [vec, others, cols, lblocks], [dfar, ffar], [*scratch, sems(2)]
        )
        return [known, *near, fblock], brought

    wide_far = pltpu.HBM(wide.shape, jnp.float32)
    resid, dblock, state, message = kernel(
        first_kernel,
        [flat, like(dfar), flat, wide_far],
        [],
        [right_side[0], zfar, dfar],
        [like(zfar), small, wide, sems(3 + nvec // ROWS)],
    )
    arrived = everywhere(message)[:, 0, :]
    state, held, lblocks, cols = smooth(state, resid, dblock, lfar, cfar)
    packed = [vmem((shape[0] * ffar.shape[2] // (BITS * lanes), lanes))] * BITS
    first, *parts = kernel(
        functools.partial(direction_kernel, count), [flat, *packed], [state, arrived, *held]
    )
    terms, (dblock,) = apply(first, parts, lblocks, cols)
    first_image, state, message = kernel(
        image_kernel, [flat, flat, wide_far], [*terms, resid, held[0], dblock], [], [small, wide, sems(1)]
    )
    arrived = everywhere(message)[:, 0, :]
    state, held, _, _ = smooth(state, first_image, dblock, lblocks, cols)
    second, rest, alpha, *parts = kernel(
        functools.partial(next_direction_kernel, count),
        [flat, flat, vmem((ROWS, lanes)), *packed],
        [state, arrived, *held, first, resid, first_image],
    )
    terms, _ = apply(second, parts, lblocks, cols, True)
    image, message = kernel(last_image_kernel, [flat, parcel], [*terms, rest], [], [small])
    arrived = everywhere(message)
    return pl.pallas_call(
        functools.partial(final_kernel, nvec, count),
        out_shape=[jax.ShapeDtypeStruct((1, *shape), jnp.float32)] * 2,
        in_specs=[pl.BlockSpec(memory_space=pltpu.VMEM)] * 6,
        compiler_params=pltpu.CompilerParams(vmem_limit_bytes=SCOPED),
    )(*[pltpu.with_memory_space_constraint(a, pltpu.VMEM) for a in (arrived, alpha, first, second, rest, image)])


def solution(mesh):
    placed = (
        P("sub", None, "coarse"),
        P("sub", None, None, None, "coarse"),
        P("sub", None, None, "coarse"),
        P("sub", None, None, "coarse"),
        P("sub", None, "coarse"),
        P("sub", None, None, "coarse"),
        P("sub", None),
    )
    return jax.shard_map(
        functools.partial(local, mesh.shape["sub"], mesh.shape["coarse"]),
        mesh=mesh,
        in_specs=placed,
        out_specs=(P("sub", None, "coarse"), P("sub", None, "coarse")),
        check_vma=False,
    )
```

```python
import functools

import jax
import jax.numpy as jnp
from jax import lax
from jax.experimental import pallas as pl
from jax.experimental.pallas import tpu as pltpu
from jax.sharding import PartitionSpec as P

SWEEPS = 3
ITERS = 2
BITS = 3
ROWS = 8
WIDE = 3
SCOPED = 6 << 20
HIGH = lax.Precision.HIGHEST


def kernel(body, outs, near, far=(), scratch=()):
    near = [pltpu.with_memory_space_constraint(a, pltpu.VMEM) for a in near]
    far = [pltpu.with_memory_space_constraint(a, pltpu.HBM) for a in far]
    there, here = pl.BlockSpec(memory_space=pl.ANY), pl.BlockSpec(memory_space=pltpu.VMEM)
    return pl.pallas_call(
        body,
        out_shape=outs,
        in_specs=[here] * len(near) + [there] * len(far),
        out_specs=[there if o.memory_space == pltpu.HBM else here for o in outs],
        scratch_shapes=scratch,
        cost_estimate=pl.CostEstimate(flops=0, bytes_accessed=0, transcendentals=0),
        compiler_params=pltpu.CompilerParams(vmem_limit_bytes=SCOPED),
    )(*near, *far)


def vmem(shape, dtype=jnp.float32):
    return pltpu.VMEM(tuple(shape), dtype)


def start_all(sources, targets, done, first=0):
    copies = [
        pltpu.make_async_copy(source, target, done.at[first + at])
        for at, (source, target) in enumerate(zip(sources, targets))
    ]
    for copy in copies:
        copy.start()
    return copies


def wait_all(copies):
    for copy in copies:
        copy.wait()


def by_rows(count, body):
    for start in range(0, count, ROWS):
        body(start)


def folded(terms):
    row = lax.broadcasted_iota(jnp.int32, terms[0].shape, 0)
    for step in (4, 2, 1):
        half = len(terms) // 2
        keep = (row & step) == 0
        terms = [
            jnp.where(keep, a, b)
            + jnp.where(keep, pltpu.roll(a, ROWS - step, 0), pltpu.roll(b, step, 0))
            for a, b in zip(terms[:half], terms[half:])
        ]
    return terms[0]


def rows_times(start, *pairs):
    terms = []
    for at in range(start, start + ROWS):
        term = None
        for blocks, vec in pairs:
            for low in range(0, vec.shape[0], 2 * ROWS):
                chunk = blocks[at, low : low + 2 * ROWS, :].astype(jnp.float32)
                upper = chunk[:ROWS] * vec[low : low + ROWS]
                term = upper if term is None else term + upper
                term = term + chunk[ROWS:] * vec[low + ROWS : low + 2 * ROWS]
        terms.append(term)
    return folded(terms)


def block_product(blocks, vec, out):
    def body(start):
        out[pl.ds(start, ROWS), :] = rows_times(start, (blocks, vec))

    by_rows(blocks.shape[0], body)


def relaxed(dblock, vec, out, base=None):
    whole = vec[...]

    def body(start):
        here = pl.ds(start, ROWS)
        part = 0.25 * (2.0 * vec[here, :] - 0.25 * rows_times(start, (dblock, whole)))
        out[here, :] = part if base is None else base[here, :] + part

    by_rows(dblock.shape[0], body)


def dot_rows(left, right):
    return jnp.sum(left * right, axis=0, keepdims=True)


def post(message, scratch):
    sub = lax.axis_index("sub")
    lanes = scratch.shape[1]
    nvec = scratch.shape[0] - ROWS
    groups = lanes // nvec
    sums = jnp.broadcast_to(jnp.sum(scratch[...], axis=1, keepdims=True), scratch.shape)
    lane = lax.broadcasted_iota(jnp.int32, scratch.shape, 1)
    row = lax.broadcasted_iota(jnp.int32, scratch.shape, 0)
    place = lax.rem(sub + row // nvec, groups) * nvec + lax.rem(row, nvec)
    line = jnp.sum(jnp.where(lane == place, sums, 0.0), axis=0, keepdims=True)
    if len(message.shape) == 3:
        message[...] = jnp.broadcast_to(line[None], message.shape)
    else:
        message[...] = jnp.broadcast_to(line, message.shape)


def inner_products(scratch, resid, image):
    nvec = scratch.shape[0] - ROWS
    scratch[nvec:, :] = jnp.concatenate(
        [dot_rows(resid, image), dot_rows(image, image), jnp.zeros((ROWS - 2, image.shape[1]), jnp.float32)], axis=0
    )


def total(x):
    return jnp.sum(x, keepdims=True)


def step_size(arrived, nvec, count):
    lane = lax.broadcasted_iota(jnp.int32, arrived.shape, 1)
    sender = lax.broadcasted_iota(jnp.int32, arrived.shape, 0)
    groups = arrived.shape[1] // nvec
    values = jnp.where(lane // nvec == lax.rem(sender // count + 1, groups), arrived[...], 0.0)
    place = lax.rem(lane, nvec)
    cross = total(jnp.where(place == 0, values, 0.0))
    square = total(jnp.where(place == 1, values, 0.0))
    return cross / (square + 1e-06)


def restriction_rows(arrived, nvec, count):
    lanes = arrived.shape[1]
    each = count * (lanes // nvec)
    lane = lax.broadcasted_iota(jnp.int32, (each, lanes), 1)
    sender = lax.broadcasted_iota(jnp.int32, (each, lanes), 0)
    keep = lane // nvec == sender // count
    return [
        jnp.sum(jnp.where(keep, arrived[at : at + each, :], 0.0), axis=0, keepdims=True)
        for at in range(0, arrived.shape[0], each)
    ]


def weights_here(inverse, rows):
    lanes = rows[0].shape[1]
    acc = inverse[:, :lanes] * rows[0]
    for at in range(1, len(rows)):
        acc = acc + inverse[:, at * lanes : (at + 1) * lanes] * rows[at]
    return jnp.broadcast_to(jnp.sum(acc, axis=1, keepdims=True), acc.shape)


def combined(weights, zvec, value):
    for at in range(weights.shape[0]):
        value = value + weights[at : at + 1, :] * zvec[at].astype(jnp.float32)
    return value


def picked(vec, others, cols, part):
    me = lax.axis_index("coarse")
    width = vec.shape[1]
    index = jnp.broadcast_to(cols[pl.ds(part, 1), :], vec.shape)
    owner = index // width
    place = lax.rem(index, width)

    def lanes(block):
        return jnp.take_along_axis(block, place, axis=1, mode="promise_in_bounds")

    if others.shape[0] == 1:
        return jnp.where(owner == me, lanes(vec[...]), lanes(others[0]))
    value = lanes(others[0])
    for at in range(1, others.shape[0]):
        value = jnp.where(owner == at, lanes(others[at]), value)
    return value


def off_rows(lblocks, chosen, start):
    return rows_times(start, *[(lblocks.at[part], vec) for part, vec in enumerate(chosen)])


def with_interface(known, vec, fblock, out):
    width = fblock.shape[2]
    vec = vec[:, :width]

    def body(start):
        here = pl.ds(start, ROWS)
        add = rows_times(start, (fblock, vec))
        pad = jnp.zeros((ROWS, out.shape[1] - width), jnp.float32)
        out[here, :] = known[here, :] + jnp.concatenate([add, pad], axis=1)

    by_rows(out.shape[0], body)


def first_kernel(resid_far, zvec_far, dblock_far, resid, dblock, state, message_far, zvec, scratch, message, done):
    pieces = [pl.ds(at, ROWS) for at in range(0, zvec.shape[0], ROWS)]
    copies = start_all(
        [resid_far, *[zvec_far.at[piece] for piece in pieces], dblock_far],
        [resid, *[zvec.at[piece] for piece in pieces], dblock],
        done,
    )
    copies[0].wait()
    vec = resid[...]
    for copy, piece in zip(copies[1:-1], pieces):
        copy.wait()
        scratch[piece, :] = rows_times(piece.start, (zvec, vec))
    scratch[zvec.shape[0] :, :] = jnp.zeros((ROWS, vec.shape[1]), jnp.float32)
    post(message, scratch)
    sent = start_all((message,), (message_far,), done, len(copies))
    copies[-1].wait()
    relaxed(dblock, resid, state)
    wait_all(sent)


def diag_kernel(vec, dblock, *refs):
    count = (len(refs) - 2) // 2
    copies = start_all(refs[:count], refs[count + 1 : -1], refs[-1])
    block_product(dblock, vec[...], refs[count])
    wait_all(copies)


def diag_copy_kernel(vec, dblock, *refs):
    count = (len(refs) - 3) // 2
    copies = start_all(refs[:count], refs[count + 2 : -1], refs[-1])
    out, copied = refs[count : count + 2]
    whole = vec[...]

    def body(start):
        rows = pl.ds(start, ROWS)
        out[rows, :] = rows_times(start, (dblock, whole))
        copied[rows] = dblock[rows]

    by_rows(out.shape[0], body)
    wait_all(copies)


def apply_kernel(vec, others, cols, lblocks, dblock_far, fblock_far, out, fblock, dblock, done):
    copies = start_all((dblock_far, fblock_far), (dblock, fblock), done)
    chosen = [picked(vec, others, cols, part) for part in range(lblocks.shape[0])]
    whole = vec[...]

    def off(start):
        out[pl.ds(start, ROWS), :] = off_rows(lblocks, chosen, start)

    def own(start):
        rows = pl.ds(start, ROWS)
        out[rows, :] = out[rows, :] + rows_times(start, (dblock, whole))

    by_rows(out.shape[0], off)
    copies[0].wait()
    by_rows(out.shape[0], own)
    copies[1].wait()


def sweep_kernel(state, others, own, resid, dblock, lblocks, cols, out, rest):
    chosen = [picked(state, others, cols, part) for part in range(lblocks.shape[0])]

    def body(start):
        here = pl.ds(start, ROWS)
        rest[here, :] = resid[here, :] - (own[here, :] + off_rows(lblocks, chosen, start))

    by_rows(dblock.shape[0], body)
    relaxed(dblock, rest, out, state)


def direction_kernel(count, state, arrived, zvec, inverse, out, *parts):
    rows = restriction_rows(arrived, zvec.shape[0], count)
    value = combined(weights_here(inverse, rows), zvec, state[...])
    out[...] = value
    pack_lanes(value, parts)


def pack_lanes(vec, parts):
    deep, lanes = vec.shape
    rows = parts[0].shape[0]
    groups = deep // rows
    inner = lanes // groups
    group = lax.broadcasted_iota(jnp.int32, (rows, lanes), 1) // inner
    for q, part in enumerate(parts):
        value = jnp.zeros((rows, lanes), jnp.float32)
        for g in range(groups):
            value = jnp.where(group == g, turned(vec[g * rows : (g + 1) * rows, :], (g - q) * inner), value)
        part[...] = value


def turned(value, lanes):
    lanes %= value.shape[1]
    return pltpu.roll(value, lanes, 1) if lanes else value


def near_lanes(parts, deep):
    rows, lanes = parts[0].shape
    groups = deep // rows
    inner = lanes // groups
    group = lax.broadcasted_iota(jnp.int32, (rows, lanes), 1) // inner
    pieces = []
    for g in range(groups):
        value = jnp.zeros((rows, lanes), jnp.float32)
        for q, part in enumerate(parts):
            value = jnp.where(group == q, turned(part[...], (q - g) * inner), value)
        pieces.append(value)
    return jnp.concatenate(pieces, axis=0)


def image_kernel(known, near0, near1, near2, fblock, resid, zvec, dblock, image, state, message_far, scratch, message, done):
    with_interface(known, near_lanes((near0, near1, near2), known.shape[0]), fblock, image)
    value = image[...]
    block_product(zvec, value, scratch)
    inner_products(scratch, resid[...], value)
    post(message, scratch)
    copies = start_all((message,), (message_far,), done)
    relaxed(dblock, image, state)
    wait_all(copies)


def next_direction_kernel(count, state, arrived, zvec, inverse, first, resid, image, out, rest, alpha, *parts):
    size = step_size(arrived, zvec.shape[0], count)
    rows = restriction_rows(arrived, zvec.shape[0], count)
    value = first[...] - size * combined(weights_here(inverse, rows), zvec, state[...])
    out[...] = value
    pack_lanes(value, parts)
    rest[...] = resid[...] - size * image[...]
    alpha[...] = jnp.broadcast_to(size, alpha.shape)


def last_image_kernel(known, near0, near1, near2, fblock, resid, image, message, scratch):
    with_interface(known, near_lanes((near0, near1, near2), known.shape[0]), fblock, image)
    scratch[...] = jnp.zeros(scratch.shape, jnp.float32)
    inner_products(scratch, resid[...], image[...])
    post(message, scratch)


def final_kernel(nvec, count, arrived, alpha, first, second, resid, image, field, rest):
    size = step_size(arrived, nvec, count)
    field[0] = alpha[0:1, :] * first[...] + size * second[...]
    rest[0] = resid[...] - size * image[...]


def swap(count, apart):
    return [(low, low ^ apart) for low in range(count) if low ^ apart < count]


def gathered(array, count):
    if count == 2:
        return lax.ppermute(array, "coarse", swap(2, 1))[None]
    return lax.all_gather(array, "coarse", axis=0)


def local(subs, count, right_side, local_blocks, diag_blocks, iface_blocks, block_cols, basis, coarse_inverse):
    lfar, dfar, ffar = local_blocks[0], diag_blocks[0], iface_blocks[0]
    cfar, zfar = block_cols[0], basis[0]
    shape = right_side.shape[1:]
    nvec, lanes = zfar.shape[0], shape[1]
    flat, small, parcel = vmem(shape), vmem((nvec + ROWS, lanes)), vmem((subs * count, lanes))
    wide = vmem((subs * count, WIDE, lanes))

    def sems(number):
        return pltpu.SemaphoreType.DMA((number,))

    def like(array, space=vmem):
        return space(array.shape, array.dtype)

    def everywhere(message):
        return lax.all_to_all(message, ("sub", "coarse"), 0, 0, tiled=len(message.shape) == 2)

    def sweep(state, others, own, resid, dblock, lblocks, cols):
        (out,) = kernel(sweep_kernel, [flat], [state, others, own, resid, dblock, lblocks, cols], (), [flat])
        return out

    def diag(vec, dblock, *far):
        return kernel(diag_kernel, [flat, *map(like, far)], [vec, dblock], far, [sems(max(len(far), 1))])

    def smooth(state, resid, dblock, lblocks, cols, *far):
        others = gathered(state, count)
        own, dblock, *more = kernel(
            diag_copy_kernel,
            [flat, like(dblock), *map(like, far)],
            [state, dblock],
            far,
            [sems(max(len(far), 1))],
        )
        lblocks, cols = more or (lblocks, cols)
        state = sweep(state, others, own, resid, dblock, lblocks, cols)
        for at in range(SWEEPS - 2):
            others = gathered(state, count)
            own, *held = diag(state, dblock, *((zfar, coarse_inverse) if at == SWEEPS - 3 else ()))
            state = sweep(state, others, own, resid, dblock, lblocks, cols)
        return state, held, lblocks, cols

    def apply(vec, parts, lblocks, cols, last=False):
        others = gathered(vec, count)
        near = [lax.ppermute(part, "sub", swap(subs, 1 << bit)) for bit, part in enumerate(parts)]
        outs, scratch = [flat, like(ffar)], [like(dfar)]
        if not last:
            outs, scratch = outs + scratch, []
        known, fblock, *brought = kernel(
            apply_kernel, outs, [vec, others, cols, lblocks], [dfar, ffar], [*scratch, sems(2)]
        )
        return [known, *near, fblock], brought

    wide_far = pltpu.HBM(wide.shape, jnp.float32)
    resid, dblock, state, message = kernel(
        first_kernel,
        [flat, like(dfar), flat, wide_far],
        [],
        [right_side[0], zfar, dfar],
        [like(zfar), small, wide, sems(3 + nvec // ROWS)],
    )
    arrived = everywhere(message)[:, 0, :]
    state, held, lblocks, cols = smooth(state, resid, dblock, lfar, cfar)
    packed = [vmem((shape[0] * ffar.shape[2] // (BITS * lanes), lanes))] * BITS
    first, *parts = kernel(
        functools.partial(direction_kernel, count), [flat, *packed], [state, arrived, *held]
    )
    terms, (dblock,) = apply(first, parts, lblocks, cols)
    first_image, state, message = kernel(
        image_kernel, [flat, flat, wide_far], [*terms, resid, held[0], dblock], [], [small, wide, sems(1)]
    )
    arrived = everywhere(message)[:, 0, :]
    state, held, _, _ = smooth(state, first_image, dblock, lblocks, cols)
    second, rest, alpha, *parts = kernel(
        functools.partial(next_direction_kernel, count),
        [flat, flat, vmem((ROWS, lanes)), *packed],
        [state, arrived, *held, first, resid, first_image],
    )
    terms, _ = apply(second, parts, lblocks, cols, True)
    image, message = kernel(last_image_kernel, [flat, parcel], [*terms, rest], [], [small])
    arrived = everywhere(message)
    return pl.pallas_call(
        functools.partial(final_kernel, nvec, count),
        out_shape=[jax.ShapeDtypeStruct((1, *shape), jnp.float32)] * 2,
        in_specs=[pl.BlockSpec(memory_space=pltpu.VMEM)] * 6,
        compiler_params=pltpu.CompilerParams(vmem_limit_bytes=SCOPED),
    )(*[pltpu.with_memory_space_constraint(a, pltpu.VMEM) for a in (arrived, alpha, first, second, rest, image)])


def solution(mesh):
    placed = (
        P("sub", None, "coarse"),
        P("sub", None, None, None, "coarse"),
        P("sub", None, None, "coarse"),
        P("sub", None, None, "coarse"),
        P("sub", None, "coarse"),
        P("sub", None, None, "coarse"),
        P("sub", None),
    )
    return jax.shard_map(
        functools.partial(local, mesh.shape["sub"], mesh.shape["coarse"]),
        mesh=mesh,
        in_specs=placed,
        out_specs=(P("sub", None, "coarse"), P("sub", None, "coarse")),
        check_vma=False,
    )
```

```python
import functools

import jax
import jax.numpy as jnp
from jax import lax
from jax.experimental import pallas as pl
from jax.experimental.pallas import tpu as pltpu
from jax.sharding import PartitionSpec as P

SWEEPS = 3
ITERS = 2
BITS = 3
ROWS = 8
SCOPED = 6 << 20
BESIDE = 1 << 30
HIGH = lax.Precision.HIGHEST


def kernel(body, outs, near, far=(), scratch=(), cost=0):
    near = [pltpu.with_memory_space_constraint(a, pltpu.VMEM) for a in near]
    far = [pltpu.with_memory_space_constraint(a, pltpu.HBM) for a in far]
    there, here = pl.BlockSpec(memory_space=pl.ANY), pl.BlockSpec(memory_space=pltpu.VMEM)
    return pl.pallas_call(
        body,
        out_shape=outs,
        in_specs=[here] * len(near) + [there] * len(far),
        out_specs=[there if o.memory_space == pltpu.HBM else here for o in outs],
        scratch_shapes=scratch,
        cost_estimate=pl.CostEstimate(flops=cost, bytes_accessed=cost, transcendentals=0),
        compiler_params=pltpu.CompilerParams(vmem_limit_bytes=SCOPED),
    )(*near, *far)


def vmem(shape, dtype=jnp.float32):
    return pltpu.VMEM(tuple(shape), dtype)


def start_all(sources, targets, done, first=0):
    copies = [
        pltpu.make_async_copy(source, target, done.at[first + at])
        for at, (source, target) in enumerate(zip(sources, targets))
    ]
    for copy in copies:
        copy.start()
    return copies


def wait_all(copies):
    for copy in copies:
        copy.wait()


def by_rows(count, body):
    for start in range(0, count, ROWS):
        body(start)


def folded(terms):
    row = lax.broadcasted_iota(jnp.int32, terms[0].shape, 0)
    for step in (4, 2, 1):
        half = len(terms) // 2
        keep = (row & step) == 0
        terms = [
            jnp.where(keep, a, b)
            + jnp.where(keep, pltpu.roll(a, ROWS - step, 0), pltpu.roll(b, step, 0))
            for a, b in zip(terms[:half], terms[half:])
        ]
    return terms[0]


def rows_times(start, *pairs):
    terms = []
    for at in range(start, start + ROWS):
        term = None
        for blocks, vec in pairs:
            for low in range(0, vec.shape[0], 2 * ROWS):
                chunk = blocks[at, low : low + 2 * ROWS, :].astype(jnp.float32)
                upper = chunk[:ROWS] * vec[low : low + ROWS]
                term = upper if term is None else term + upper
                term = term + chunk[ROWS:] * vec[low + ROWS : low + 2 * ROWS]
        terms.append(term)
    return folded(terms)


def block_product(blocks, vec, out):
    def body(start):
        out[pl.ds(start, ROWS), :] = rows_times(start, (blocks, vec))

    by_rows(blocks.shape[0], body)


def relaxed(dblock, vec, out, base=None, copied=None):
    whole = vec[...]

    def body(start):
        here = pl.ds(start, ROWS)
        part = 0.25 * (2.0 * vec[here, :] - 0.25 * rows_times(start, (dblock, whole)))
        out[here, :] = part if base is None else base[here, :] + part
        if copied is not None:
            copied[here] = dblock[here]

    by_rows(dblock.shape[0], body)


def dot_rows(left, right):
    return jnp.sum(left * right, axis=0, keepdims=True)


def post(message, scratch):
    sub = lax.axis_index("sub")
    lanes = scratch.shape[1]
    nvec = scratch.shape[0] - ROWS
    groups = lanes // nvec
    sums = jnp.broadcast_to(jnp.sum(scratch[...], axis=1, keepdims=True), scratch.shape)
    lane = lax.broadcasted_iota(jnp.int32, scratch.shape, 1)
    row = lax.broadcasted_iota(jnp.int32, scratch.shape, 0)
    place = lax.rem(sub + row // nvec, groups) * nvec + lax.rem(row, nvec)
    line = jnp.sum(jnp.where(lane == place, sums, 0.0), axis=0, keepdims=True)
    message[...] = jnp.broadcast_to(line, message.shape)


def inner_products(scratch, resid, image):
    nvec = scratch.shape[0] - ROWS
    scratch[nvec:, :] = jnp.concatenate(
        [dot_rows(resid, image), dot_rows(image, image), jnp.zeros((ROWS - 2, image.shape[1]), jnp.float32)], axis=0
    )


def total(x):
    return jnp.sum(x, keepdims=True)


def step_size(arrived, nvec, count):
    lane = lax.broadcasted_iota(jnp.int32, arrived.shape, 1)
    sender = lax.broadcasted_iota(jnp.int32, arrived.shape, 0)
    groups = arrived.shape[1] // nvec
    values = jnp.where(lane // nvec == lax.rem(sender // count + 1, groups), arrived[...], 0.0)
    place = lax.rem(lane, nvec)
    cross = total(jnp.where(place == 0, values, 0.0))
    square = total(jnp.where(place == 1, values, 0.0))
    return cross / (square + 1e-06)


def restriction_rows(arrived, nvec, count):
    lanes = arrived.shape[1]
    each = count * (lanes // nvec)
    lane = lax.broadcasted_iota(jnp.int32, (each, lanes), 1)
    sender = lax.broadcasted_iota(jnp.int32, (each, lanes), 0)
    keep = lane // nvec == sender // count
    return [
        jnp.sum(jnp.where(keep, arrived[at : at + each, :], 0.0), axis=0, keepdims=True)
        for at in range(0, arrived.shape[0], each)
    ]


def weights_here(inverse, rows):
    lanes = rows[0].shape[1]
    acc = inverse[:, :lanes] * rows[0]
    for at in range(1, len(rows)):
        acc = acc + inverse[:, at * lanes : (at + 1) * lanes] * rows[at]
    return jnp.broadcast_to(jnp.sum(acc, axis=1, keepdims=True), acc.shape)


def combined(weights, zvec, value):
    for at in range(weights.shape[0]):
        value = value + weights[at : at + 1, :] * zvec[at].astype(jnp.float32)
    return value


def picked(vec, others, cols, part):
    me = lax.axis_index("coarse")
    width = vec.shape[1]
    index = jnp.broadcast_to(cols[pl.ds(part, 1), :], vec.shape)
    owner = index // width
    place = lax.rem(index, width)

    def lanes(block):
        return jnp.take_along_axis(block, place, axis=1, mode="promise_in_bounds")

    if others.shape[0] == 1:
        return jnp.where(owner == me, lanes(vec[...]), lanes(others[0]))
    value = lanes(others[0])
    for at in range(1, others.shape[0]):
        value = jnp.where(owner == at, lanes(others[at]), value)
    return value


def off_rows(lblocks, chosen, start):
    return rows_times(start, *[(lblocks.at[part], vec) for part, vec in enumerate(chosen)])


def with_interface(known, vec, fblock, out):
    width = fblock.shape[2]
    vec = vec[:, :width]

    def body(start):
        here = pl.ds(start, ROWS)
        add = rows_times(start, (fblock, vec))
        pad = jnp.zeros((ROWS, out.shape[1] - width), jnp.float32)
        out[here, :] = known[here, :] + jnp.concatenate([add, pad], axis=1)

    by_rows(out.shape[0], body)


def first_kernel(resid_far, zvec_far, dblock_far, resid, dblock, state, message_far, zvec, scratch, message, done):
    pieces = [pl.ds(at, ROWS) for at in range(0, zvec.shape[0], ROWS)]
    copies = start_all(
        [resid_far, *[zvec_far.at[piece] for piece in pieces], dblock_far],
        [resid, *[zvec.at[piece] for piece in pieces], dblock],
        done,
    )
    copies[0].wait()
    vec = resid[...]
    for copy, piece in zip(copies[1:-1], pieces):
        copy.wait()
        scratch[piece, :] = rows_times(piece.start, (zvec, vec))
    scratch[zvec.shape[0] :, :] = jnp.zeros((ROWS, vec.shape[1]), jnp.float32)
    post(message, scratch)
    sent = start_all((message,), (message_far,), done, len(copies))
    copies[-1].wait()
    relaxed(dblock, resid, state)
    wait_all(sent)


def diag_kernel(vec, dblock, *refs):
    count = (len(refs) - 2) // 2
    copies = start_all(refs[:count], refs[count + 1 : -1], refs[-1])
    block_product(dblock, vec[...], refs[count])
    wait_all(copies)


def apply_kernel(vec, others, cols, lblocks, dblock_far, fblock_far, out, fblock, dblock, done):
    copies = start_all((dblock_far, fblock_far), (dblock, fblock), done)
    chosen = [picked(vec, others, cols, part) for part in range(lblocks.shape[0])]
    whole = vec[...]

    def off(start):
        out[pl.ds(start, ROWS), :] = off_rows(lblocks, chosen, start)

    def own(start):
        rows = pl.ds(start, ROWS)
        out[rows, :] = out[rows, :] + rows_times(start, (dblock, whole))

    by_rows(out.shape[0], off)
    copies[0].wait()
    by_rows(out.shape[0], own)
    copies[1].wait()


def sweep_kernel(state, others, own, resid, dblock, lblocks, cols, out, *refs):
    *copied, rest = refs
    chosen = [picked(state, others, cols, part) for part in range(lblocks.shape[0])]

    def body(start):
        here = pl.ds(start, ROWS)
        rest[here, :] = resid[here, :] - (own[here, :] + off_rows(lblocks, chosen, start))

    by_rows(dblock.shape[0], body)
    relaxed(dblock, rest, out, state, *copied)


def direction_kernel(count, state, arrived, zvec, inverse, out, *parts):
    rows = restriction_rows(arrived, zvec.shape[0], count)
    value = combined(weights_here(inverse, rows), zvec, state[...])
    out[...] = value
    pack_lanes(value, parts)


def pack_lanes(vec, parts):
    deep, lanes = vec.shape
    rows = parts[0].shape[0]
    groups = deep // rows
    inner = lanes // groups
    group = lax.broadcasted_iota(jnp.int32, (rows, lanes), 1) // inner
    for q, part in enumerate(parts):
        value = jnp.zeros((rows, lanes), jnp.float32)
        for g in range(groups):
            value = jnp.where(group == g, turned(vec[g * rows : (g + 1) * rows, :], (g - q) * inner), value)
        part[...] = value


def turned(value, lanes):
    lanes %= value.shape[1]
    return pltpu.roll(value, lanes, 1) if lanes else value


def near_lanes(parts, deep):
    rows, lanes = parts[0].shape
    groups = deep // rows
    inner = lanes // groups
    group = lax.broadcasted_iota(jnp.int32, (rows, lanes), 1) // inner
    pieces = []
    for g in range(groups):
        value = jnp.zeros((rows, lanes), jnp.float32)
        for q, part in enumerate(parts):
            value = jnp.where(group == q, turned(part[...], (q - g) * inner), value)
        pieces.append(value)
    return jnp.concatenate(pieces, axis=0)


def image_kernel(known, near0, near1, near2, fblock, resid, zvec, dblock, image, state, message_far, scratch, message, done):
    with_interface(known, near_lanes((near0, near1, near2), known.shape[0]), fblock, image)
    value = image[...]
    block_product(zvec, value, scratch)
    inner_products(scratch, resid[...], value)
    post(message, scratch)
    copies = start_all((message,), (message_far,), done)
    relaxed(dblock, image, state)
    wait_all(copies)


def next_direction_kernel(count, state, arrived, zvec, inverse, first, resid, image, out, rest, alpha, *parts):
    size = step_size(arrived, zvec.shape[0], count)
    rows = restriction_rows(arrived, zvec.shape[0], count)
    value = first[...] - size * combined(weights_here(inverse, rows), zvec, state[...])
    out[...] = value
    pack_lanes(value, parts)
    rest[...] = resid[...] - size * image[...]
    alpha[...] = jnp.broadcast_to(size, alpha.shape)


def last_image_kernel(known, near0, near1, near2, fblock, resid, dblock, image, message, scratch):
    with_interface(known, near_lanes((near0, near1, near2), known.shape[0]), fblock, image)
    scratch[...] = jnp.zeros(scratch.shape, jnp.float32)
    inner_products(scratch, resid[...], image[...])
    post(message, scratch)


def final_kernel(nvec, count, arrived, alpha, first, second, resid, image, field, rest):
    size = step_size(arrived, nvec, count)
    field[0] = alpha[0:1, :] * first[...] + size * second[...]
    rest[0] = resid[...] - size * image[...]


def swap(count, apart):
    return [(low, low ^ apart) for low in range(count) if low ^ apart < count]


def gathered(array, count):
    if count == 2:
        return lax.ppermute(array, "coarse", swap(2, 1))[None]
    return lax.all_gather(array, "coarse", axis=0)


def local(subs, count, right_side, local_blocks, diag_blocks, iface_blocks, block_cols, basis, coarse_inverse):
    lfar, dfar, ffar = local_blocks[0], diag_blocks[0], iface_blocks[0]
    cfar, zfar = block_cols[0], basis[0]
    shape = right_side.shape[1:]
    nvec, lanes = zfar.shape[0], shape[1]
    flat, small, parcel = vmem(shape), vmem((nvec + ROWS, lanes)), vmem((subs * count, lanes))

    def sems(number):
        return pltpu.SemaphoreType.DMA((number,))

    def like(array, space=vmem):
        return space(array.shape, array.dtype)

    def everywhere(message):
        return lax.all_to_all(message, ("sub", "coarse"), 0, 0, tiled=True)

    def sweep(*args, copy=False):
        return kernel(sweep_kernel, [flat, like(dfar)] if copy else [flat], args, (), [flat])

    def diag(vec, dblock, far=(), cost=0):
        return kernel(diag_kernel, [flat, *map(like, far)], [vec, dblock], far, [sems(max(len(far), 1))], cost)

    def smooth(state, resid, dblock, lblocks, cols, cost=0):
        others = gathered(state, count)
        (own,) = diag(state, dblock, (), cost)
        state, dblock = sweep(state, others, own, resid, dblock, lblocks, cols, copy=True)
        for at in range(SWEEPS - 2):
            others = gathered(state, count)
            own, *held = diag(state, dblock, (zfar, coarse_inverse) if at == SWEEPS - 3 else (), BESIDE)
            (state,) = sweep(state, others, own, resid, dblock, lblocks, cols)
        return state, held

    def apply(vec, parts, lblocks, cols):
        others = gathered(vec, count)
        near = [lax.ppermute(part, "sub", swap(subs, 1 << bit)) for bit, part in enumerate(parts)]
        known, fblock, dblock = kernel(
            apply_kernel, [flat, like(ffar), like(dfar)], [vec, others, cols, lblocks], [dfar, ffar], [sems(2)]
        )
        return [known, *near, fblock], dblock

    parcel_far = pltpu.HBM(parcel.shape, jnp.float32)
    resid, dblock, state, message = kernel(
        first_kernel,
        [flat, like(dfar), flat, parcel_far],
        [],
        [right_side[0], zfar, dfar],
        [like(zfar), small, parcel, sems(3 + nvec // ROWS)],
    )
    arrived = everywhere(message)
    lblocks, cols = lfar, cfar
    state, held = smooth(state, resid, dblock, lblocks, cols, BESIDE)
    packed = [vmem((shape[0] * ffar.shape[2] // (BITS * lanes), lanes))] * BITS
    first, *parts = kernel(
        functools.partial(direction_kernel, count), [flat, *packed], [state, arrived, *held]
    )
    terms, dblock = apply(first, parts, lblocks, cols)
    first_image, state, message = kernel(
        image_kernel, [flat, flat, parcel_far], [*terms, resid, held[0], dblock], [], [small, parcel, sems(1)]
    )
    arrived = everywhere(message)
    state, held = smooth(state, first_image, dblock, lblocks, cols)
    second, rest, alpha, *parts = kernel(
        functools.partial(next_direction_kernel, count),
        [flat, flat, vmem((ROWS, lanes)), *packed],
        [state, arrived, *held, first, resid, first_image],
    )
    terms, dblock = apply(second, parts, lblocks, cols)
    image, message = kernel(last_image_kernel, [flat, parcel], [*terms, rest, dblock], [], [small])
    arrived = everywhere(message)
    return pl.pallas_call(
        functools.partial(final_kernel, nvec, count),
        out_shape=[jax.ShapeDtypeStruct((1, *shape), jnp.float32)] * 2,
        in_specs=[pl.BlockSpec(memory_space=pltpu.VMEM)] * 6,
        compiler_params=pltpu.CompilerParams(vmem_limit_bytes=SCOPED),
    )(*[pltpu.with_memory_space_constraint(a, pltpu.VMEM) for a in (arrived, alpha, first, second, rest, image)])


def solution(mesh):
    placed = (
        P("sub", None, "coarse"),
        P("sub", None, None, None, "coarse"),
        P("sub", None, None, "coarse"),
        P("sub", None, None, "coarse"),
        P("sub", None, "coarse"),
        P("sub", None, None, "coarse"),
        P("sub", None),
    )
    return jax.shard_map(
        functools.partial(local, mesh.shape["sub"], mesh.shape["coarse"]),
        mesh=mesh,
        in_specs=placed,
        out_specs=(P("sub", None, "coarse"), P("sub", None, "coarse")),
        check_vma=False,
    )
```

```python
import functools

import jax
import jax.numpy as jnp
from jax import lax
from jax.experimental import pallas as pl
from jax.experimental.pallas import tpu as pltpu
from jax.sharding import PartitionSpec as P

SWEEPS = 3
ITERS = 2
BITS = 3
ROWS = 8
SCOPED = 6 << 20
BESIDE = 1 << 30
HIGH = lax.Precision.HIGHEST


def kernel(body, outs, near, far=(), scratch=(), cost=0):
    near = [pltpu.with_memory_space_constraint(a, pltpu.VMEM) for a in near]
    far = [pltpu.with_memory_space_constraint(a, pltpu.HBM) for a in far]
    there, here = pl.BlockSpec(memory_space=pl.ANY), pl.BlockSpec(memory_space=pltpu.VMEM)
    return pl.pallas_call(
        body,
        out_shape=outs,
        in_specs=[here] * len(near) + [there] * len(far),
        out_specs=[there if o.memory_space == pltpu.HBM else here for o in outs],
        scratch_shapes=scratch,
        cost_estimate=pl.CostEstimate(flops=cost, bytes_accessed=cost, transcendentals=0),
        compiler_params=pltpu.CompilerParams(vmem_limit_bytes=SCOPED),
    )(*near, *far)


def vmem(shape, dtype=jnp.float32):
    return pltpu.VMEM(tuple(shape), dtype)


def start_all(sources, targets, done, first=0):
    copies = [
        pltpu.make_async_copy(source, target, done.at[first + at])
        for at, (source, target) in enumerate(zip(sources, targets))
    ]
    for copy in copies:
        copy.start()
    return copies


def wait_all(copies):
    for copy in copies:
        copy.wait()


def by_rows(count, body):
    for start in range(0, count, ROWS):
        body(start)


def folded(terms):
    row = lax.broadcasted_iota(jnp.int32, terms[0].shape, 0)
    for step in (4, 2, 1):
        half = len(terms) // 2
        keep = (row & step) == 0
        terms = [
            jnp.where(keep, a, b)
            + jnp.where(keep, pltpu.roll(a, ROWS - step, 0), pltpu.roll(b, step, 0))
            for a, b in zip(terms[:half], terms[half:])
        ]
    return terms[0]


def rows_times(start, *pairs):
    terms = []
    for at in range(start, start + ROWS):
        term = None
        for blocks, vec in pairs:
            for low in range(0, vec.shape[0], 2 * ROWS):
                chunk = blocks[at, low : low + 2 * ROWS, :].astype(jnp.float32)
                upper = chunk[:ROWS] * vec[low : low + ROWS]
                term = upper if term is None else term + upper
                term = term + chunk[ROWS:] * vec[low + ROWS : low + 2 * ROWS]
        terms.append(term)
    return folded(terms)


def block_product(blocks, vec, out):
    def body(start):
        out[pl.ds(start, ROWS), :] = rows_times(start, (blocks, vec))

    by_rows(blocks.shape[0], body)


def relaxed(dblock, vec, out, base=None, copied=None):
    whole = vec[...]

    def body(start):
        here = pl.ds(start, ROWS)
        part = 0.25 * (2.0 * vec[here, :] - 0.25 * rows_times(start, (dblock, whole)))
        out[here, :] = part if base is None else base[here, :] + part
        if copied is not None:
            copied[here] = dblock[here]

    by_rows(dblock.shape[0], body)


def dot_rows(left, right):
    return jnp.sum(left * right, axis=0, keepdims=True)


def post(message, scratch):
    sub = lax.axis_index("sub")
    lanes = scratch.shape[1]
    nvec = scratch.shape[0] - ROWS
    groups = lanes // nvec
    sums = jnp.broadcast_to(jnp.sum(scratch[...], axis=1, keepdims=True), scratch.shape)
    lane = lax.broadcasted_iota(jnp.int32, scratch.shape, 1)
    row = lax.broadcasted_iota(jnp.int32, scratch.shape, 0)
    place = lax.rem(sub + row // nvec, groups) * nvec + lax.rem(row, nvec)
    line = jnp.sum(jnp.where(lane == place, sums, 0.0), axis=0, keepdims=True)
    message[...] = jnp.broadcast_to(line, message.shape)


def inner_products(scratch, resid, image):
    nvec = scratch.shape[0] - ROWS
    scratch[nvec:, :] = jnp.concatenate(
        [dot_rows(resid, image), dot_rows(image, image), jnp.zeros((ROWS - 2, image.shape[1]), jnp.float32)], axis=0
    )


def total(x):
    return jnp.sum(x, keepdims=True)


def step_size(arrived, nvec, count):
    lane = lax.broadcasted_iota(jnp.int32, arrived.shape, 1)
    sender = lax.broadcasted_iota(jnp.int32, arrived.shape, 0)
    groups = arrived.shape[1] // nvec
    values = jnp.where(lane // nvec == lax.rem(sender // count + 1, groups), arrived[...], 0.0)
    place = lax.rem(lane, nvec)
    cross = total(jnp.where(place == 0, values, 0.0))
    square = total(jnp.where(place == 1, values, 0.0))
    return cross / (square + 1e-06)


def restriction_rows(arrived, nvec, count):
    lanes = arrived.shape[1]
    each = count * (lanes // nvec)
    lane = lax.broadcasted_iota(jnp.int32, (each, lanes), 1)
    sender = lax.broadcasted_iota(jnp.int32, (each, lanes), 0)
    keep = lane // nvec == sender // count
    return [
        jnp.sum(jnp.where(keep, arrived[at : at + each, :], 0.0), axis=0, keepdims=True)
        for at in range(0, arrived.shape[0], each)
    ]


def weights_here(inverse, rows):
    lanes = rows[0].shape[1]
    acc = inverse[:, :lanes] * rows[0]
    for at in range(1, len(rows)):
        acc = acc + inverse[:, at * lanes : (at + 1) * lanes] * rows[at]
    return jnp.broadcast_to(jnp.sum(acc, axis=1, keepdims=True), acc.shape)


def combined(weights, zvec, value):
    for at in range(weights.shape[0]):
        value = value + weights[at : at + 1, :] * zvec[at].astype(jnp.float32)
    return value


def picked(vec, others, cols, part):
    me = lax.axis_index("coarse")
    width = vec.shape[1]
    index = jnp.broadcast_to(cols[pl.ds(part, 1), :], vec.shape)
    owner = index // width
    place = lax.rem(index, width)

    def lanes(block):
        return jnp.take_along_axis(block, place, axis=1, mode="promise_in_bounds")

    if others.shape[0] == 1:
        return jnp.where(owner == me, lanes(vec[...]), lanes(others[0]))
    value = lanes(others[0])
    for at in range(1, others.shape[0]):
        value = jnp.where(owner == at, lanes(others[at]), value)
    return value


def off_rows(lblocks, chosen, start):
    return rows_times(start, *[(lblocks.at[part], vec) for part, vec in enumerate(chosen)])


def with_interface(known, vec, fblock, out):
    width = fblock.shape[2]
    vec = vec[:, :width]

    def body(start):
        here = pl.ds(start, ROWS)
        add = rows_times(start, (fblock, vec))
        pad = jnp.zeros((ROWS, out.shape[1] - width), jnp.float32)
        out[here, :] = known[here, :] + jnp.concatenate([add, pad], axis=1)

    by_rows(out.shape[0], body)


def first_kernel(resid_far, zvec_far, dblock_far, resid, dblock, state, message_far, zvec, scratch, message, done):
    pieces = [pl.ds(at, ROWS) for at in range(0, zvec.shape[0], ROWS)]
    copies = start_all(
        [resid_far, *[zvec_far.at[piece] for piece in pieces], dblock_far],
        [resid, *[zvec.at[piece] for piece in pieces], dblock],
        done,
    )
    copies[0].wait()
    vec = resid[...]
    for copy, piece in zip(copies[1:-1], pieces):
        copy.wait()
        scratch[piece, :] = rows_times(piece.start, (zvec, vec))
    scratch[zvec.shape[0] :, :] = jnp.zeros((ROWS, vec.shape[1]), jnp.float32)
    post(message, scratch)
    sent = start_all((message,), (message_far,), done, len(copies))
    copies[-1].wait()
    relaxed(dblock, resid, state)
    wait_all(sent)


def diag_kernel(vec, dblock, *refs):
    count = (len(refs) - 2) // 2
    copies = start_all(refs[:count], refs[count + 1 : -1], refs[-1])
    block_product(dblock, vec[...], refs[count])
    wait_all(copies)


def apply_kernel(vec, others, cols, lblocks, dblock_far, fblock_far, out, fblock, dblock, done):
    copies = start_all((dblock_far, fblock_far), (dblock, fblock), done)
    chosen = [picked(vec, others, cols, part) for part in range(lblocks.shape[0])]
    whole = vec[...]

    def off(start):
        out[pl.ds(start, ROWS), :] = off_rows(lblocks, chosen, start)

    def own(start):
        rows = pl.ds(start, ROWS)
        out[rows, :] = out[rows, :] + rows_times(start, (dblock, whole))

    by_rows(out.shape[0], off)
    copies[0].wait()
    by_rows(out.shape[0], own)
    copies[1].wait()


def sweep_kernel(state, others, own, resid, dblock, lblocks, cols, out, *refs):
    *copied, rest = refs
    chosen = [picked(state, others, cols, part) for part in range(lblocks.shape[0])]

    def body(start):
        here = pl.ds(start, ROWS)
        rest[here, :] = resid[here, :] - (own[here, :] + off_rows(lblocks, chosen, start))

    by_rows(dblock.shape[0], body)
    relaxed(dblock, rest, out, state, *copied)


def direction_kernel(count, state, arrived, zvec, inverse, out, *parts):
    rows = restriction_rows(arrived, zvec.shape[0], count)
    value = combined(weights_here(inverse, rows), zvec, state[...])
    out[...] = value
    pack_lanes(value, parts)


def pack_lanes(vec, parts):
    deep, lanes = vec.shape
    rows = parts[0].shape[0]
    groups = deep // rows
    inner = lanes // groups
    group = lax.broadcasted_iota(jnp.int32, (rows, lanes), 1) // inner
    for q, part in enumerate(parts):
        value = jnp.zeros((rows, lanes), jnp.float32)
        for g in range(groups):
            value = jnp.where(group == g, turned(vec[g * rows : (g + 1) * rows, :], (g - q) * inner), value)
        part[...] = value


def turned(value, lanes):
    lanes %= value.shape[1]
    return pltpu.roll(value, lanes, 1) if lanes else value


def near_lanes(parts, deep):
    rows, lanes = parts[0].shape
    groups = deep // rows
    inner = lanes // groups
    group = lax.broadcasted_iota(jnp.int32, (rows, lanes), 1) // inner
    pieces = []
    for g in range(groups):
        value = jnp.zeros((rows, lanes), jnp.float32)
        for q, part in enumerate(parts):
            value = jnp.where(group == q, turned(part[...], (q - g) * inner), value)
        pieces.append(value)
    return jnp.concatenate(pieces, axis=0)


def image_kernel(known, near0, near1, near2, fblock, resid, zvec, dblock, image, state, own, message_far, scratch, message, done):
    with_interface(known, near_lanes((near0, near1, near2), known.shape[0]), fblock, image)
    value = image[...]
    block_product(zvec, value, scratch)
    inner_products(scratch, resid[...], value)
    post(message, scratch)
    copies = start_all((message,), (message_far,), done)
    relaxed(dblock, image, state)
    block_product(dblock, state[...], own)
    wait_all(copies)


def next_direction_kernel(count, state, arrived, zvec, inverse, first, resid, image, out, rest, alpha, *parts):
    size = step_size(arrived, zvec.shape[0], count)
    rows = restriction_rows(arrived, zvec.shape[0], count)
    value = first[...] - size * combined(weights_here(inverse, rows), zvec, state[...])
    out[...] = value
    pack_lanes(value, parts)
    rest[...] = resid[...] - size * image[...]
    alpha[...] = jnp.broadcast_to(size, alpha.shape)


def last_image_kernel(known, near0, near1, near2, fblock, resid, dblock, image, message, scratch):
    with_interface(known, near_lanes((near0, near1, near2), known.shape[0]), fblock, image)
    scratch[...] = jnp.zeros(scratch.shape, jnp.float32)
    inner_products(scratch, resid[...], image[...])
    post(message, scratch)


def final_kernel(nvec, count, arrived, alpha, first, second, resid, image, field, rest):
    size = step_size(arrived, nvec, count)
    field[0] = alpha[0:1, :] * first[...] + size * second[...]
    rest[0] = resid[...] - size * image[...]


def swap(count, apart):
    return [(low, low ^ apart) for low in range(count) if low ^ apart < count]


def gathered(array, count):
    if count == 2:
        return lax.ppermute(array, "coarse", swap(2, 1))[None]
    return lax.all_gather(array, "coarse", axis=0)


def local(subs, count, right_side, local_blocks, diag_blocks, iface_blocks, block_cols, basis, coarse_inverse):
    lfar, dfar, ffar = local_blocks[0], diag_blocks[0], iface_blocks[0]
    cfar, zfar = block_cols[0], basis[0]
    shape = right_side.shape[1:]
    nvec, lanes = zfar.shape[0], shape[1]
    flat, small, parcel = vmem(shape), vmem((nvec + ROWS, lanes)), vmem((subs * count, lanes))

    def sems(number):
        return pltpu.SemaphoreType.DMA((number,))

    def like(array, space=vmem):
        return space(array.shape, array.dtype)

    def everywhere(message):
        return lax.all_to_all(message, ("sub", "coarse"), 0, 0, tiled=True)

    def sweep(*args, copy=False):
        return kernel(sweep_kernel, [flat, like(dfar)] if copy else [flat], args, (), [flat])

    def diag(vec, dblock, far=(), cost=0):
        return kernel(diag_kernel, [flat, *map(like, far)], [vec, dblock], far, [sems(max(len(far), 1))], cost)

    def smooth(state, resid, dblock, lblocks, cols, own=None):
        others = gathered(state, count)
        if own is None:
            (own,) = diag(state, dblock, (), BESIDE)
        state, dblock = sweep(state, others, own, resid, dblock, lblocks, cols, copy=True)
        for at in range(SWEEPS - 2):
            others = gathered(state, count)
            own, *held = diag(state, dblock, (zfar, coarse_inverse) if at == SWEEPS - 3 else (), BESIDE)
            (state,) = sweep(state, others, own, resid, dblock, lblocks, cols)
        return state, held

    def apply(vec, parts, lblocks, cols):
        others = gathered(vec, count)
        near = [lax.ppermute(part, "sub", swap(subs, 1 << bit)) for bit, part in enumerate(parts)]
        known, fblock, dblock = kernel(
            apply_kernel, [flat, like(ffar), like(dfar)], [vec, others, cols, lblocks], [dfar, ffar], [sems(2)]
        )
        return [known, *near, fblock], dblock

    parcel_far = pltpu.HBM(parcel.shape, jnp.float32)
    resid, dblock, state, message = kernel(
        first_kernel,
        [flat, like(dfar), flat, parcel_far],
        [],
        [right_side[0], zfar, dfar],
        [like(zfar), small, parcel, sems(3 + nvec // ROWS)],
    )
    arrived = everywhere(message)
    lblocks, cols = lfar, cfar
    state, held = smooth(state, resid, dblock, lblocks, cols)
    packed = [vmem((shape[0] * ffar.shape[2] // (BITS * lanes), lanes))] * BITS
    first, *parts = kernel(
        functools.partial(direction_kernel, count), [flat, *packed], [state, arrived, *held]
    )
    terms, dblock = apply(first, parts, lblocks, cols)
    first_image, state, own, message = kernel(
        image_kernel, [flat, flat, flat, parcel_far], [*terms, resid, held[0], dblock], [], [small, parcel, sems(1)]
    )
    arrived = everywhere(message)
    state, held = smooth(state, first_image, dblock, lblocks, cols, own)
    second, rest, alpha, *parts = kernel(
        functools.partial(next_direction_kernel, count),
        [flat, flat, vmem((ROWS, lanes)), *packed],
        [state, arrived, *held, first, resid, first_image],
    )
    terms, dblock = apply(second, parts, lblocks, cols)
    image, message = kernel(last_image_kernel, [flat, parcel], [*terms, rest, dblock], [], [small])
    arrived = everywhere(message)
    return pl.pallas_call(
        functools.partial(final_kernel, nvec, count),
        out_shape=[jax.ShapeDtypeStruct((1, *shape), jnp.float32)] * 2,
        in_specs=[pl.BlockSpec(memory_space=pltpu.VMEM)] * 6,
        compiler_params=pltpu.CompilerParams(vmem_limit_bytes=SCOPED),
    )(*[pltpu.with_memory_space_constraint(a, pltpu.VMEM) for a in (arrived, alpha, first, second, rest, image)])


def solution(mesh):
    placed = (
        P("sub", None, "coarse"),
        P("sub", None, None, None, "coarse"),
        P("sub", None, None, "coarse"),
        P("sub", None, None, "coarse"),
        P("sub", None, "coarse"),
        P("sub", None, None, "coarse"),
        P("sub", None),
    )
    return jax.shard_map(
        functools.partial(local, mesh.shape["sub"], mesh.shape["coarse"]),
        mesh=mesh,
        in_specs=placed,
        out_specs=(P("sub", None, "coarse"), P("sub", None, "coarse")),
        check_vma=False,
    )
```

```python
import functools

import jax
import jax.numpy as jnp
from jax import lax
from jax.experimental import pallas as pl
from jax.experimental.pallas import tpu as pltpu
from jax.sharding import PartitionSpec as P

SWEEPS = 3
ITERS = 2
BITS = 3
ROWS = 8
SCOPED = 6 << 20
BESIDE = 1 << 30
HIGH = lax.Precision.HIGHEST


def kernel(body, outs, near, far=(), scratch=(), cost=0):
    near = [pltpu.with_memory_space_constraint(a, pltpu.VMEM) for a in near]
    far = [pltpu.with_memory_space_constraint(a, pltpu.HBM) for a in far]
    there, here = pl.BlockSpec(memory_space=pl.ANY), pl.BlockSpec(memory_space=pltpu.VMEM)
    return pl.pallas_call(
        body,
        out_shape=outs,
        in_specs=[here] * len(near) + [there] * len(far),
        out_specs=[there if o.memory_space == pltpu.HBM else here for o in outs],
        scratch_shapes=scratch,
        cost_estimate=pl.CostEstimate(flops=cost, bytes_accessed=cost, transcendentals=0),
        compiler_params=pltpu.CompilerParams(vmem_limit_bytes=SCOPED),
    )(*near, *far)


def vmem(shape, dtype=jnp.float32):
    return pltpu.VMEM(tuple(shape), dtype)


def start_all(sources, targets, done, first=0):
    copies = [
        pltpu.make_async_copy(source, target, done.at[first + at])
        for at, (source, target) in enumerate(zip(sources, targets))
    ]
    for copy in copies:
        copy.start()
    return copies


def wait_all(copies):
    for copy in copies:
        copy.wait()


def by_rows(count, body):
    for start in range(0, count, ROWS):
        body(start)


def folded(terms):
    row = lax.broadcasted_iota(jnp.int32, terms[0].shape, 0)
    for step in (4, 2, 1):
        half = len(terms) // 2
        keep = (row & step) == 0
        terms = [
            jnp.where(keep, a, b)
            + jnp.where(keep, pltpu.roll(a, ROWS - step, 0), pltpu.roll(b, step, 0))
            for a, b in zip(terms[:half], terms[half:])
        ]
    return terms[0]


def rows_times(start, *pairs):
    terms = []
    for at in range(start, start + ROWS):
        term = None
        for blocks, vec in pairs:
            for low in range(0, vec.shape[0], 2 * ROWS):
                chunk = blocks[at, low : low + 2 * ROWS, :].astype(jnp.float32)
                upper = chunk[:ROWS] * vec[low : low + ROWS]
                term = upper if term is None else term + upper
                term = term + chunk[ROWS:] * vec[low + ROWS : low + 2 * ROWS]
        terms.append(term)
    return folded(terms)


def block_product(blocks, vec, out):
    def body(start):
        out[pl.ds(start, ROWS), :] = rows_times(start, (blocks, vec))

    by_rows(blocks.shape[0], body)


def relaxed(dblock, vec, out, base=None, copied=None):
    whole = vec[...]

    def body(start):
        here = pl.ds(start, ROWS)
        part = 0.25 * (2.0 * vec[here, :] - 0.25 * rows_times(start, (dblock, whole)))
        out[here, :] = part if base is None else base[here, :] + part
        if copied is not None:
            copied[here] = dblock[here]

    by_rows(dblock.shape[0], body)


def dot_rows(left, right):
    return jnp.sum(left * right, axis=0, keepdims=True)


def post(message, scratch):
    sub = lax.axis_index("sub")
    lanes = scratch.shape[1]
    nvec = scratch.shape[0] - ROWS
    groups = lanes // nvec
    sums = jnp.broadcast_to(jnp.sum(scratch[...], axis=1, keepdims=True), scratch.shape)
    lane = lax.broadcasted_iota(jnp.int32, scratch.shape, 1)
    row = lax.broadcasted_iota(jnp.int32, scratch.shape, 0)
    place = lax.rem(sub + row // nvec, groups) * nvec + lax.rem(row, nvec)
    line = jnp.sum(jnp.where(lane == place, sums, 0.0), axis=0, keepdims=True)
    message[...] = jnp.broadcast_to(line, message.shape)


def inner_products(scratch, resid, image):
    nvec = scratch.shape[0] - ROWS
    scratch[nvec:, :] = jnp.concatenate(
        [dot_rows(resid, image), dot_rows(image, image), jnp.zeros((ROWS - 2, image.shape[1]), jnp.float32)], axis=0
    )


def total(x):
    return jnp.sum(x, keepdims=True)


def step_size(arrived, nvec, count):
    lane = lax.broadcasted_iota(jnp.int32, arrived.shape, 1)
    sender = lax.broadcasted_iota(jnp.int32, arrived.shape, 0)
    groups = arrived.shape[1] // nvec
    values = jnp.where(lane // nvec == lax.rem(sender // count + 1, groups), arrived[...], 0.0)
    line = jnp.sum(values, axis=0, keepdims=True)
    place = lax.rem(lane[:ROWS], nvec)
    pair = jnp.sum(jnp.where(place == sender[:ROWS], line, 0.0), axis=1, keepdims=True)
    return pair[0:1] / (pair[1:2] + 1e-06)


def restriction_rows(arrived, nvec, count):
    lanes = arrived.shape[1]
    each = count * (lanes // nvec)
    lane = lax.broadcasted_iota(jnp.int32, (each, lanes), 1)
    sender = lax.broadcasted_iota(jnp.int32, (each, lanes), 0)
    keep = lane // nvec == sender // count
    return [
        jnp.sum(jnp.where(keep, arrived[at : at + each, :], 0.0), axis=0, keepdims=True)
        for at in range(0, arrived.shape[0], each)
    ]


def weights_here(inverse, rows):
    lanes = rows[0].shape[1]
    acc = inverse[:, :lanes] * rows[0]
    for at in range(1, len(rows)):
        acc = acc + inverse[:, at * lanes : (at + 1) * lanes] * rows[at]
    return jnp.broadcast_to(jnp.sum(acc, axis=1, keepdims=True), acc.shape)


def combined(weights, zvec, value):
    for at in range(weights.shape[0]):
        value = value + weights[at : at + 1, :] * zvec[at].astype(jnp.float32)
    return value


def picked(vec, others, cols, part):
    me = lax.axis_index("coarse")
    width = vec.shape[1]
    index = jnp.broadcast_to(cols[pl.ds(part, 1), :], vec.shape)
    owner = index // width
    place = lax.rem(index, width)

    def lanes(block):
        return jnp.take_along_axis(block, place, axis=1, mode="promise_in_bounds")

    if others.shape[0] == 1:
        return jnp.where(owner == me, lanes(vec[...]), lanes(others[0]))
    value = lanes(others[0])
    for at in range(1, others.shape[0]):
        value = jnp.where(owner == at, lanes(others[at]), value)
    return value


def off_rows(lblocks, chosen, start):
    return rows_times(start, *[(lblocks.at[part], vec) for part, vec in enumerate(chosen)])


def with_interface(known, vec, fblock, out):
    width = fblock.shape[2]
    vec = vec[:, :width]

    def body(start):
        here = pl.ds(start, ROWS)
        add = rows_times(start, (fblock, vec))
        pad = jnp.zeros((ROWS, out.shape[1] - width), jnp.float32)
        out[here, :] = known[here, :] + jnp.concatenate([add, pad], axis=1)

    by_rows(out.shape[0], body)


def first_kernel(resid_far, zvec_far, dblock_far, resid, dblock, state, message_far, zvec, scratch, message, done):
    pieces = [pl.ds(at, ROWS) for at in range(0, zvec.shape[0], ROWS)]
    copies = start_all(
        [resid_far, *[zvec_far.at[piece] for piece in pieces], dblock_far],
        [resid, *[zvec.at[piece] for piece in pieces], dblock],
        done,
    )
    copies[0].wait()
    vec = resid[...]
    for copy, piece in zip(copies[1:-1], pieces):
        copy.wait()
        scratch[piece, :] = rows_times(piece.start, (zvec, vec))
    scratch[zvec.shape[0] :, :] = jnp.zeros((ROWS, vec.shape[1]), jnp.float32)
    post(message, scratch)
    sent = start_all((message,), (message_far,), done, len(copies))
    copies[-1].wait()
    relaxed(dblock, resid, state)
    wait_all(sent)


def diag_kernel(vec, dblock, *refs):
    count = (len(refs) - 2) // 2
    copies = start_all(refs[:count], refs[count + 1 : -1], refs[-1])
    block_product(dblock, vec[...], refs[count])
    wait_all(copies)


def apply_kernel(vec, others, cols, lblocks, dblock_far, fblock_far, out, fblock, dblock, done):
    copies = start_all((dblock_far, fblock_far), (dblock, fblock), done)
    chosen = [picked(vec, others, cols, part) for part in range(lblocks.shape[0])]
    whole = vec[...]

    def off(start):
        out[pl.ds(start, ROWS), :] = off_rows(lblocks, chosen, start)

    def own(start):
        rows = pl.ds(start, ROWS)
        out[rows, :] = out[rows, :] + rows_times(start, (dblock, whole))

    by_rows(out.shape[0], off)
    copies[0].wait()
    by_rows(out.shape[0], own)
    copies[1].wait()


def sweep_kernel(state, others, own, resid, dblock, lblocks, cols, out, *refs):
    *copied, rest = refs
    chosen = [picked(state, others, cols, part) for part in range(lblocks.shape[0])]

    def body(start):
        here = pl.ds(start, ROWS)
        rest[here, :] = resid[here, :] - (own[here, :] + off_rows(lblocks, chosen, start))

    by_rows(dblock.shape[0], body)
    relaxed(dblock, rest, out, state, *copied)


def direction_kernel(count, state, arrived, zvec, inverse, out, *parts):
    rows = restriction_rows(arrived, zvec.shape[0], count)
    value = combined(weights_here(inverse, rows), zvec, state[...])
    out[...] = value
    pack_lanes(value, parts)


def pack_lanes(vec, parts):
    deep, lanes = vec.shape
    rows = parts[0].shape[0]
    groups = deep // rows
    inner = lanes // groups
    group = lax.broadcasted_iota(jnp.int32, (rows, lanes), 1) // inner
    for q, part in enumerate(parts):
        value = jnp.zeros((rows, lanes), jnp.float32)
        for g in range(groups):
            value = jnp.where(group == g, turned(vec[g * rows : (g + 1) * rows, :], (g - q) * inner), value)
        part[...] = value


def turned(value, lanes):
    lanes %= value.shape[1]
    return pltpu.roll(value, lanes, 1) if lanes else value


def near_lanes(parts, deep):
    rows, lanes = parts[0].shape
    groups = deep // rows
    inner = lanes // groups
    group = lax.broadcasted_iota(jnp.int32, (rows, lanes), 1) // inner
    pieces = []
    for g in range(groups):
        value = jnp.zeros((rows, lanes), jnp.float32)
        for q, part in enumerate(parts):
            value = jnp.where(group == q, turned(part[...], (q - g) * inner), value)
        pieces.append(value)
    return jnp.concatenate(pieces, axis=0)


def image_kernel(known, near0, near1, near2, fblock, resid, zvec, dblock, image, state, own, message_far, scratch, message, done):
    with_interface(known, near_lanes((near0, near1, near2), known.shape[0]), fblock, image)
    value = image[...]
    block_product(zvec, value, scratch)
    inner_products(scratch, resid[...], value)
    post(message, scratch)
    copies = start_all((message,), (message_far,), done)
    relaxed(dblock, image, state)
    block_product(dblock, state[...], own)
    wait_all(copies)


def next_direction_kernel(count, state, arrived, zvec, inverse, first, resid, image, out, rest, alpha, *parts):
    size = step_size(arrived, zvec.shape[0], count)
    rows = restriction_rows(arrived, zvec.shape[0], count)
    value = first[...] - size * combined(weights_here(inverse, rows), zvec, state[...])
    out[...] = value
    pack_lanes(value, parts)
    rest[...] = resid[...] - size * image[...]
    alpha[...] = jnp.broadcast_to(size, alpha.shape)


def last_image_kernel(known, near0, near1, near2, fblock, resid, dblock, image, message, scratch):
    with_interface(known, near_lanes((near0, near1, near2), known.shape[0]), fblock, image)
    scratch[...] = jnp.zeros(scratch.shape, jnp.float32)
    inner_products(scratch, resid[...], image[...])
    post(message, scratch)


def final_kernel(nvec, count, arrived, alpha, first, second, resid, image, field, rest):
    size = step_size(arrived, nvec, count)
    field[0] = alpha[0:1, :] * first[...] + size * second[...]
    rest[0] = resid[...] - size * image[...]


def swap(count, apart):
    return [(low, low ^ apart) for low in range(count) if low ^ apart < count]


def gathered(array, count):
    if count == 2:
        return lax.ppermute(array, "coarse", swap(2, 1))[None]
    return lax.all_gather(array, "coarse", axis=0)


def local(subs, count, right_side, local_blocks, diag_blocks, iface_blocks, block_cols, basis, coarse_inverse):
    lfar, dfar, ffar = local_blocks[0], diag_blocks[0], iface_blocks[0]
    cfar, zfar = block_cols[0], basis[0]
    shape = right_side.shape[1:]
    nvec, lanes = zfar.shape[0], shape[1]
    flat, small, parcel = vmem(shape), vmem((nvec + ROWS, lanes)), vmem((subs * count, lanes))

    def sems(number):
        return pltpu.SemaphoreType.DMA((number,))

    def like(array, space=vmem):
        return space(array.shape, array.dtype)

    def everywhere(message):
        return lax.all_to_all(message, ("sub", "coarse"), 0, 0, tiled=True)

    def sweep(*args, copy=False):
        return kernel(sweep_kernel, [flat, like(dfar)] if copy else [flat], args, (), [flat])

    def diag(vec, dblock, far=(), cost=0):
        return kernel(diag_kernel, [flat, *map(like, far)], [vec, dblock], far, [sems(max(len(far), 1))], cost)

    def smooth(state, resid, dblock, lblocks, cols, own=None):
        others = gathered(state, count)
        if own is None:
            (own,) = diag(state, dblock, (), BESIDE)
        state, dblock = sweep(state, others, own, resid, dblock, lblocks, cols, copy=True)
        for at in range(SWEEPS - 2):
            others = gathered(state, count)
            own, *held = diag(state, dblock, (zfar, coarse_inverse) if at == SWEEPS - 3 else (), BESIDE)
            (state,) = sweep(state, others, own, resid, dblock, lblocks, cols)
        return state, held

    def apply(vec, parts, lblocks, cols):
        others = gathered(vec, count)
        near = [lax.ppermute(part, "sub", swap(subs, 1 << bit)) for bit, part in enumerate(parts)]
        known, fblock, dblock = kernel(
            apply_kernel, [flat, like(ffar), like(dfar)], [vec, others, cols, lblocks], [dfar, ffar], [sems(2)]
        )
        return [known, *near, fblock], dblock

    parcel_far = pltpu.HBM(parcel.shape, jnp.float32)
    resid, dblock, state, message = kernel(
        first_kernel,
        [flat, like(dfar), flat, parcel_far],
        [],
        [right_side[0], zfar, dfar],
        [like(zfar), small, parcel, sems(3 + nvec // ROWS)],
    )
    arrived = everywhere(message)
    lblocks, cols = lfar, cfar
    state, held = smooth(state, resid, dblock, lblocks, cols)
    packed = [vmem((shape[0] * ffar.shape[2] // (BITS * lanes), lanes))] * BITS
    first, *parts = kernel(
        functools.partial(direction_kernel, count), [flat, *packed], [state, arrived, *held]
    )
    terms, dblock = apply(first, parts, lblocks, cols)
    first_image, state, own, message = kernel(
        image_kernel, [flat, flat, flat, parcel_far], [*terms, resid, held[0], dblock], [], [small, parcel, sems(1)]
    )
    arrived = everywhere(message)
    state, held = smooth(state, first_image, dblock, lblocks, cols, own)
    second, rest, alpha, *parts = kernel(
        functools.partial(next_direction_kernel, count),
        [flat, flat, vmem((ROWS, lanes)), *packed],
        [state, arrived, *held, first, resid, first_image],
    )
    terms, dblock = apply(second, parts, lblocks, cols)
    image, message = kernel(last_image_kernel, [flat, parcel], [*terms, rest, dblock], [], [small])
    arrived = everywhere(message)
    return pl.pallas_call(
        functools.partial(final_kernel, nvec, count),
        out_shape=[jax.ShapeDtypeStruct((1, *shape), jnp.float32)] * 2,
        in_specs=[pl.BlockSpec(memory_space=pltpu.VMEM)] * 6,
        compiler_params=pltpu.CompilerParams(vmem_limit_bytes=SCOPED),
    )(*[pltpu.with_memory_space_constraint(a, pltpu.VMEM) for a in (arrived, alpha, first, second, rest, image)])


def solution(mesh):
    placed = (
        P("sub", None, "coarse"),
        P("sub", None, None, None, "coarse"),
        P("sub", None, None, "coarse"),
        P("sub", None, None, "coarse"),
        P("sub", None, "coarse"),
        P("sub", None, None, "coarse"),
        P("sub", None),
    )
    return jax.shard_map(
        functools.partial(local, mesh.shape["sub"], mesh.shape["coarse"]),
        mesh=mesh,
        in_specs=placed,
        out_specs=(P("sub", None, "coarse"), P("sub", None, "coarse")),
        check_vma=False,
    )
```
